32 devices in a mesh: dp: 4 (over y, core), tensor: 8 (over z, x).
Axes of the slice: x: 2, y: 2, z: 4, core: 2. Of those that a mesh axis runs over, the one named last changes fastest.
Arguments:
- hidden_in: bfloat16 [4, 8, 128, 2, 4096], P('dp', None, None, None, 'tensor'), may hold values from -6 to 6
- conv_weight: bfloat16 [3, 3, 2, 4096], P(None, None, None, 'tensor'), may hold values from -2 to 2
- proj_weight: bfloat16 [4096, 2048], P('tensor'), may hold values from -0.125 to 0.125
- out_grad: bfloat16 [4, 8, 128, 2048], P('dp', 'tensor'), may hold values from -6 to 6
- sample_gate: float32 [4, 2048], P('dp'), may hold values from -4 to 4
Outputs:
- hidden_grad: bfloat16 [4, 8, 128, 2, 4096], P('dp', None, None, None, 'tensor')
- proj_grad: bfloat16 [4096, 2048], P('tensor')
- conv_grad: float32 [3, 3, 2, 4096], P(None, None, None, 'tensor')
The draws below stay inside these ranges and needn't reach their ends.
All inputs are finite; a program needn't handle non-finite values.
Results may differ from the reference program's by a relative error of at most 0.0057.
Values may be sent and summed in bfloat16 or wider, within the bound.
No kernel may reach another device: no remote copies, remote signals or barrier semaphores. Data moves between devices by JAX's collectives and lax.ppermute only.
A program may use at most 128 MiB of HBM per device.

```python
import math
import jax
import jax.numpy as jnp
from jax import lax

D = 2048
HID = 4096
IMG_W = 128
IMG_H = 8
SAMPLES = 4


def block_levels(stream_key, dims, cuts, least, top_value):
    level, own = 1.0, jax.random.fold_in(stream_key, 6)
    for position, blocks in cuts:
        heights = jnp.exp(jax.random.uniform(jax.random.fold_in(own, position), (blocks,), jnp.float32, least / len(cuts), top_value / len(cuts)))
        level = level * jnp.repeat(heights, dims[position] // blocks).reshape([-1 if axis == position else 1 for axis in range(len(dims))])
    return level


def gaussian(key, dims, scale, bound, cuts=(), dtype=jnp.bfloat16):
    result = jax.random.normal(key, dims, jnp.float32) * scale
    if len(cuts) > 0:
        result = block_levels(key, dims, cuts, -0.22, 0.18) * result
    return jnp.clip(result, min=-bound, max=bound).astype(dtype)


def setup_inputs(seed: int = 0) -> dict:
    arg_keys = jax.random.split(jax.random.key(seed), 6)
    return {
        "hidden_in": gaussian(arg_keys[0], (SAMPLES, IMG_H, IMG_W, 2, HID), 1.0, 6.0, ((0, 4), (4, 8))),
        "conv_weight": gaussian(arg_keys[1], (3, 3, 2, HID), 9 ** -0.5, 2.0, ((3, 8),)),
        "proj_weight": gaussian(arg_keys[2], (HID, D), D ** -0.5, 0.125, ((0, 8),)),
        "out_grad": gaussian(arg_keys[3], (SAMPLES, IMG_H, IMG_W, D), 1.0, 6.0, ((0, 4), (1, 8))),
        "sample_gate": gaussian(arg_keys[4], (SAMPLES, D), 1.0, 4.0, ((0, 4),), jnp.float32),
    }


def depthwise(volume, kernel, mirror):
    height = volume.shape[1]
    across = volume.shape[2]
    padded = jnp.pad(volume, ((0, 0), (1, 1), (1, 1), (0, 0), (0, 0)))
    summed = jnp.zeros(volume.shape, jnp.float32)
    for i in range(3):
        for j in range(3):
            a = 2 - i if mirror else i
            b = 2 - j if mirror else j
            summed = summed + kernel[i, j].astype(jnp.float32) * padded[:, a:a + height, b:b + across]
    return summed

def kernel_terms(grad_pre, volume):
    height = volume.shape[1]
    across = volume.shape[2]
    padded = jnp.pad(volume, ((0, 0), (1, 1), (1, 1), (0, 0), (0, 0)))
    rows_out = []
    for i in range(3):
        row_terms = []
        for j in range(3):
            row_terms.append(lax.optimization_barrier(jnp.sum(grad_pre * padded[:, i:i + height, j:j + across], axis=(0, 1, 2))))
        rows_out.append(jnp.stack(row_terms))
    return jnp.stack(rows_out)

def reference(hidden_in, conv_weight, proj_weight, out_grad, sample_gate):
    grad_scale = 1.0 / math.sqrt(SAMPLES * IMG_H * IMG_W)

    def per_sample(running, inputs):
        volume, grad_rows, gate_rows = inputs
        volume = volume[None]
        gated_grad = (grad_rows.astype(jnp.float32) * gate_rows).astype(jnp.bfloat16)
        conv_out = depthwise(volume, conv_weight, False)
        value_part = conv_out[..., 0, :]
        gate_part = conv_out[..., 1, :]
        gate_sig = jax.nn.sigmoid(gate_part)
        mixed_act = (value_part * gate_part * gate_sig).astype(jnp.bfloat16)
        flat_grad = gated_grad.reshape(-1, D)
        flat_act = mixed_act.reshape(-1, HID)
        grad_mixed = jnp.dot(flat_grad, proj_weight.T, preferred_element_type=jnp.float32).reshape(mixed_act.shape)
        proj_sum = running[0] + jnp.dot(flat_act.T, flat_grad, preferred_element_type=jnp.float32)
        grad_pre = jnp.stack([grad_mixed * gate_part * gate_sig, grad_mixed * value_part * gate_sig * (1.0 + gate_part * (1.0 - gate_sig))], axis=-2)
        hidden_grad = depthwise(grad_pre, conv_weight, True).astype(jnp.bfloat16)
        kernel_sum = running[1] + kernel_terms(grad_pre, volume)
        return ((proj_sum, kernel_sum), hidden_grad[0])
    start_state = (jnp.zeros((HID, D), jnp.float32), jnp.zeros((3, 3, 2, HID), jnp.float32))
    sums, hidden_grad = lax.scan(per_sample, start_state, (hidden_in, out_grad, sample_gate))
    proj_grad = (sums[0] * grad_scale).astype(jnp.bfloat16)
    conv_grad = sums[1] * grad_scale
    return (hidden_grad, proj_grad, conv_grad)
```

```python
import functools
import math

import jax
import jax.numpy as jnp
from jax import lax
from jax.experimental import pallas as pl
from jax.experimental.pallas import tpu as pltpu
from jax.sharding import PartitionSpec as P

F32 = jnp.float32
BF16 = jnp.bfloat16
PAD = 8
TILE = 16
LANES = 128
VMEM_BYTES = 48 * 1024 * 1024


def ring_order(n):
    return [2 * i if i < n // 2 else 2 * (n - 1 - i) + 1 for i in range(n)]


def at_ring(position, n):
    position = lax.rem(position + 2 * n, n)
    return jnp.where(position < n // 2, 2 * position, 2 * (n - 1 - position) + 1)


def ring_place(index, n):
    half = index // 2
    return jnp.where(lax.rem(index, 2) == 0, half, n - 1 - half)


def split_widths(depth):
    first = depth * 5 // 8 // 256 * 256
    return [first, depth - first]


def conv_kernel(hidden_ref, weight_ref, gate_ref, value_ref, mixed_ref, pad_ref):
    _, height, across, lanes = hidden_ref.shape
    for k in range(2):
        pad_ref[k, 0] = jnp.zeros(pad_ref.shape[2:], F32)
        pad_ref[k, height + 1] = jnp.zeros(pad_ref.shape[2:], F32)

    @pl.loop(0, height)
    def _(r):
        for k in range(2):
            pad_ref[k, r + 1, 0:PAD] = jnp.zeros((PAD, lanes), F32)
            pad_ref[k, r + 1, PAD + across : 2 * PAD + across] = jnp.zeros((PAD, lanes), F32)
            pad_ref[k, r + 1, PAD : PAD + across] = hidden_ref[k, r].astype(F32)

    weights = weight_ref[...]

    @pl.loop(0, height)
    def _(r):
        for t in range(across // TILE):
            w = t * TILE
            parts = []
            for k in range(2):
                total = None
                for i in range(3):
                    for j in range(3):
                        term = (
                            weights[(i * 3 + j) * 2 + k][None, :]
                            * pad_ref[k, r + i, PAD + w + j - 1 : PAD + w + j - 1 + TILE]
                        )
                        total = term if total is None else total + term
                parts.append(total)
            value, gate = parts
            sig = 1.0 / (1.0 + jnp.exp(-gate))
            gated = gate * sig
            gate_ref[r, w : w + TILE] = gated
            value_ref[r, w : w + TILE] = value * sig * (1.0 + gate * (1.0 - sig))
            mixed_ref[r, w : w + TILE] = (value * gated).astype(BF16)


def conv_parts(hidden, weights):
    _, height, across, channels = hidden.shape
    block = pl.BlockSpec((height, across, LANES), lambda c: (0, 0, c))
    return pl.pallas_call(
        conv_kernel,
        grid=(channels // LANES,),
        in_specs=[
            pl.BlockSpec((2, height, across, LANES), lambda c: (0, 0, 0, c)),
            pl.BlockSpec((18, LANES), lambda c: (0, c)),
        ],
        out_specs=[block, block, block],
        out_shape=[
            jax.ShapeDtypeStruct((height, across, channels), F32),
            jax.ShapeDtypeStruct((height, across, channels), F32),
            jax.ShapeDtypeStruct((height, across, channels), BF16),
        ],
        scratch_shapes=[pltpu.VMEM((2, height + 2, across + 2 * PAD, LANES), F32)],
        compiler_params=pltpu.CompilerParams(vmem_limit_bytes=VMEM_BYTES),
        cost_estimate=pl.CostEstimate(
            flops=height * across * channels * 60,
            bytes_accessed=height * across * channels * 14,
            transcendentals=height * across * channels,
        ),
    )(hidden, weights)


def matmul_kernel(n, first, place_ref, *refs):
    count = n + 1
    pieces, refs = refs[:count], refs[count:]
    gate_ref, weight_ref, mixed_ref = refs[:3]
    refs = refs[3:]
    if first:
        before_ref, refs = None, refs
    else:
        before_ref, refs = refs[0], refs[1:]
    grad_ref, send_ref, keep_ref, full_ref = refs
    across = pieces[0].shape[0]
    width = pieces[0].shape[1]
    me, core = place_ref[0], place_ref[1]
    spot = ring_place(me, n)
    gate = gate_ref[...]
    starts = []
    for step in range(n // 2):
        if step == 0:
            starts.append(at_ring(spot, n) * across)
        else:
            starts.append(at_ring(spot - step, n) * across)
            starts.append(at_ring(spot + step, n) * across)
    far = at_ring(spot + n // 2, n) * across
    starts.extend([far, far + across // 2])
    for piece, start in zip(pieces, starts):
        rows = piece.shape[0]
        full_ref[pl.ds(pl.multiple_of(start, rows), rows)] = (
            piece[...].astype(F32) * gate
        ).astype(BF16)
    tokens = full_ref.shape[0]
    half = width // 2
    slab = min(tokens, 512)

    @pl.loop(0, tokens // slab)
    def _(s):
        rows = pl.ds(pl.multiple_of(s * slab, slab), slab)
        product = lax.dot_general(
            full_ref[rows], weight_ref[...], (((1,), (1,)), ((), ())), preferred_element_type=F32
        )
        if before_ref is not None:
            product = product + before_ref[rows]
        grad_ref[rows] = product

    for out_ref, column in ((send_ref, 1 - core), (keep_ref, core)):
        columns = pl.ds(pl.multiple_of(column * half, LANES), half)
        out_ref[...] = lax.dot_general(
            mixed_ref[...],
            full_ref[:, columns],
            (((0,), (0,)), ((), ())),
            preferred_element_type=F32,
        ).astype(out_ref.dtype)


def matmul_parts(n, place, pieces, gate, weight, mixed, before):
    across, width = pieces[0].shape
    channels = weight.shape[0]
    tokens = mixed.shape[0]
    first = before is None
    vmem = pl.BlockSpec(memory_space=pltpu.VMEM)
    operands = [*pieces, gate, weight, mixed] + ([] if first else [before])
    return pl.pallas_call(
        functools.partial(matmul_kernel, n, first),
        in_specs=[pl.BlockSpec(memory_space=pltpu.SMEM)] + [vmem] * len(operands),
        out_specs=[vmem] * 3,
        out_shape=[
            jax.ShapeDtypeStruct((tokens, channels), F32),
            jax.ShapeDtypeStruct((channels, width // 2), BF16),
            jax.ShapeDtypeStruct((channels, width // 2), F32),
        ],
        scratch_shapes=[pltpu.VMEM((tokens, width), BF16)],
        compiler_params=pltpu.CompilerParams(vmem_limit_bytes=VMEM_BYTES),
        cost_estimate=pl.CostEstimate(
            flops=4 * tokens * channels * width,
            bytes_accessed=tokens * width * 2 + channels * width * 5 + tokens * channels * 10,
            transcendentals=0,
        ),
    )(place, *operands)


def grads_kernel(grad_ref, gate_ref, value_ref, hidden_ref, weight_ref, out_ref, term_ref, pad_ref):
    _, height, across, lanes = hidden_ref.shape
    for k in range(2):
        pad_ref[k, 0] = jnp.zeros(pad_ref.shape[2:], F32)
        pad_ref[k, height + 1] = jnp.zeros(pad_ref.shape[2:], F32)

    @pl.loop(0, height)
    def _(r):
        grad = grad_ref[r]
        for k, factor in enumerate((gate_ref, value_ref)):
            pad_ref[k, r + 1, 0:PAD] = jnp.zeros((PAD, lanes), F32)
            pad_ref[k, r + 1, PAD + across : 2 * PAD + across] = jnp.zeros((PAD, lanes), F32)
            pad_ref[k, r + 1, PAD : PAD + across] = grad * factor[r]

    weights = weight_ref[...]
    for k in range(2):

        def row(r, sums):
            sums = list(sums)
            for t in range(across // TILE):
                w = t * TILE
                own = hidden_ref[k, r, w : w + TILE].astype(F32)
                total = None
                for i in range(3):
                    for j in range(3):
                        view = pad_ref[k, r + 2 - i, PAD + w + 1 - j : PAD + w + 1 - j + TILE]
                        term = weights[(i * 3 + j) * 2 + k][None, :] * view
                        total = term if total is None else total + term
                        both = view * own
                        sums[i * 3 + j] = sums[i * 3 + j] + (both[:8] + both[8:])
                out_ref[k, r, w : w + TILE] = total.astype(BF16)
            return tuple(sums)

        sums = lax.fori_loop(0, height, row, tuple(jnp.zeros((8, lanes), F32) for _ in range(9)))
        for tap in range(9):
            term_ref[tap * 2 + k : tap * 2 + k + 1] = jnp.sum(sums[tap], axis=0, keepdims=True)


def grads(grad, gate_part, value_part, hidden, weights):
    _, height, across, channels = hidden.shape
    block = pl.BlockSpec((height, across, LANES), lambda c: (0, 0, c))
    pair = pl.BlockSpec((2, height, across, LANES), lambda c: (0, 0, 0, c))
    taps = pl.BlockSpec((18, LANES), lambda c: (0, c))
    return pl.pallas_call(
        grads_kernel,
        grid=(channels // LANES,),
        in_specs=[block, block, block, pair, taps],
        out_specs=[pair, taps],
        out_shape=[
            jax.ShapeDtypeStruct(hidden.shape, BF16),
            jax.ShapeDtypeStruct((18, channels), F32),
        ],
        scratch_shapes=[pltpu.VMEM((2, height + 2, across + 2 * PAD, LANES), F32)],
        compiler_params=pltpu.CompilerParams(vmem_limit_bytes=VMEM_BYTES),
        cost_estimate=pl.CostEstimate(
            flops=height * across * channels * 80,
            bytes_accessed=height * across * channels * 20,
            transcendentals=0,
        ),
    )(grad, gate_part, value_part, hidden, weights)


def place_kernel(place_ref, mine_ref, other_ref, whole_ref, out_ref):
    step = pl.program_id(0)

    @pl.when(step == 0)
    def _():
        out_ref[...] = mine_ref[...]

    @pl.when(step == 1)
    def _():
        out_ref[...] = other_ref[...]


def put(place, mine, other, whole, offset):
    channels, half = mine.shape
    unit = math.gcd(half, offset) if offset else half
    return pl.pallas_call(
        place_kernel,
        grid_spec=pltpu.PrefetchScalarGridSpec(
            num_scalar_prefetch=1,
            grid=(2, half // unit),
            in_specs=[
                pl.BlockSpec((channels, unit), lambda h, u, s: (0, u)),
                pl.BlockSpec((channels, unit), lambda h, u, s: (0, u)),
                pl.BlockSpec(memory_space=pl.ANY),
            ],
            out_specs=pl.BlockSpec(
                (channels, unit),
                lambda h, u, s: (
                    0,
                    offset // unit + (h + s[1] - 2 * h * s[1]) * (half // unit) + u,
                ),
            ),
        ),
        out_shape=jax.ShapeDtypeStruct(whole.shape, whole.dtype),
        input_output_aliases={3: 0},
        compiler_params=pltpu.CompilerParams(vmem_limit_bytes=VMEM_BYTES),
        cost_estimate=pl.CostEstimate(
            flops=0, bytes_accessed=channels * half * 8, transcendentals=0
        ),
    )(place, mine, other, whole)


def ring_gather(n, own, state):
    ring = ring_order(n)
    right = [(ring[i], ring[(i + 1) % n]) for i in range(n)]
    left = [(ring[i], ring[(i - 1) % n]) for i in range(n)]
    half = own.shape[0] // 2
    gathered = [own]
    up = down = own
    for step in range(1, n // 2):
        up = lax.ppermute(up, "tensor", right)
        down = lax.ppermute(down, "tensor", left)
        gathered += [up, down]
        state.append((up, down))
    gathered.append(lax.ppermute(up[:half], "tensor", right))
    gathered.append(lax.ppermute(down[half:], "tensor", left))
    return gathered


def swap(value, bit):
    n = lax.axis_size("dp")
    return lax.ppermute(value, "dp", [(i, i ^ bit) for i in range(n)])


def sum_rest(value, low=2):
    bit = low
    while bit < lax.axis_size("dp"):
        value = value.astype(F32) + swap(value, bit).astype(F32)
        if bit * 2 < lax.axis_size("dp"):
            value = value.astype(BF16)
        bit *= 2
    return value


def on_device(hidden_in, conv_weight, proj_weight, out_grad, sample_gate):
    samples, height, across, _, channels = hidden_in.shape
    depth = out_grad.shape[-1]
    n = lax.axis_size("tensor")
    dp = lax.axis_size("dp")
    assert samples == 1 and out_grad.shape[1] == 1 and n % 2 == 0 and dp & (dp - 1) == 0
    grad_scale = 1.0 / math.sqrt(dp * samples * height * across)
    place = jnp.stack([lax.axis_index("tensor"), lax.rem(lax.axis_index("dp"), 2)]).astype(
        jnp.int32
    )
    own = out_grad.reshape(across, depth)
    hidden = jnp.transpose(hidden_in.reshape(height, across, 2, channels), (2, 0, 1, 3))
    taps = conv_weight.astype(F32).reshape(18, channels)

    widths = split_widths(depth)
    offset = 0
    chunks = []
    previous = None
    for width in widths:
        block = own[:, offset : offset + width]
        if previous is not None:
            block = lax.optimization_barrier((block, *previous[1]))[0]
        state = []
        pieces = ring_gather(n, block, state)
        previous = state
        chunks.append((offset, width, pieces))
        offset += width

    gate_part, value_part, mixed = conv_parts(hidden, taps)
    mixed = mixed.reshape(height * across, channels)
    grad = None
    whole = jnp.zeros((channels, depth), BF16)
    for offset, width, pieces in chunks:
        grad, send, keep = matmul_parts(
            n,
            place,
            pieces,
            sample_gate[:, offset : offset + width],
            proj_weight[:, offset : offset + width],
            mixed,
            grad,
        )
        pair = (keep + swap(send, 1).astype(F32)).astype(BF16)
        mine = (sum_rest(pair) * grad_scale).astype(BF16)
        other = swap(mine, 1)
        whole = put(place, mine, other, whole, offset)

    hidden_grad, terms = grads(
        grad.reshape(height, across, channels), gate_part, value_part, hidden, taps
    )
    total = terms
    bit = 1
    while bit < dp:
        total = total + swap(total, bit)
        bit *= 2
    conv_grad = (total * grad_scale).reshape(3, 3, 2, channels)
    hidden_grad = jnp.transpose(hidden_grad, (1, 2, 0, 3))[None]
    return (hidden_grad, whole, conv_grad)


def solution(mesh):
    in_specs = (
        P("dp", None, None, None, "tensor"),
        P(None, None, None, "tensor"),
        P("tensor", None),
        P("dp", "tensor", None, None),
        P("dp", None),
    )
    out_specs = (
        P("dp", None, None, None, "tensor"),
        P("tensor", None),
        P(None, None, None, "tensor"),
    )
    return jax.shard_map(
        on_device, mesh=mesh, in_specs=in_specs, out_specs=out_specs, check_vma=False
    )
```

```python
import functools
import math

import jax
import jax.numpy as jnp
from jax import lax
from jax.experimental import pallas as pl
from jax.experimental.pallas import tpu as pltpu
from jax.sharding import PartitionSpec as P

F32 = jnp.float32
BF16 = jnp.bfloat16
PAD = 8
TILE = 16
LANES = 128
VMEM_BYTES = 20 * 1024 * 1024
VMEM = pl.BlockSpec(memory_space=pltpu.VMEM)
SMEM = pl.BlockSpec(memory_space=pltpu.SMEM)


def ring_order(n):
    return [2 * i if i < n // 2 else 2 * (n - 1 - i) + 1 for i in range(n)]


def at_ring(position, n):
    position = lax.rem(position + 2 * n, n)
    return jnp.where(position < n // 2, 2 * position, 2 * (n - 1 - position) + 1)


def ring_place(index, n):
    half = index // 2
    return jnp.where(lax.rem(index, 2) == 0, half, n - 1 - half)


def split_widths(depth):
    return [depth // 2, depth // 2]


def params(limit=VMEM_BYTES):
    return pltpu.CompilerParams(vmem_limit_bytes=limit)


def cost(flops, moved, transcendentals=0):
    return pl.CostEstimate(flops=flops, bytes_accessed=moved, transcendentals=transcendentals)


def clear_edges(pad_ref, height, across):
    lanes = pad_ref.shape[-1]
    for k in range(2):
        pad_ref[k, 0] = jnp.zeros(pad_ref.shape[2:], F32)
        pad_ref[k, height + 1] = jnp.zeros(pad_ref.shape[2:], F32)

        @pl.loop(0, height)
        def _(r):
            pad_ref[k, r + 1, 0:PAD] = jnp.zeros((PAD, lanes), F32)
            pad_ref[k, r + 1, PAD + across : 2 * PAD + across] = jnp.zeros((PAD, lanes), F32)


def conv_kernel(hidden_ref, weight_ref, gate_ref, value_ref, mixed_ref, pad_ref):
    _, height, across, channels = hidden_ref.shape
    clear_edges(pad_ref, height, across)

    @pl.loop(0, channels // LANES)
    def _(c):
        lanes = pl.ds(pl.multiple_of(c * LANES, LANES), LANES)

        @pl.loop(0, height)
        def _(r):
            for k in range(2):
                pad_ref[k, r + 1, PAD : PAD + across] = hidden_ref[k, r, :, lanes].astype(F32)

        weights = weight_ref[:, lanes]

        @pl.loop(0, height)
        def _(r):
            mixed = []
            for t in range(across // TILE):
                w = t * TILE
                parts = []
                for k in range(2):
                    total = None
                    for i in range(3):
                        for j in range(3):
                            view = pad_ref[k, r + i, PAD + w + j - 1 : PAD + w + j - 1 + TILE]
                            term = weights[(i * 3 + j) * 2 + k][None, :] * view
                            total = term if total is None else total + term
                    parts.append(total)
                value, gate = parts
                sig = 1.0 / (1.0 + jnp.exp(-gate))
                gated = gate * sig
                gate_ref[r, w : w + TILE, lanes] = gated.astype(BF16)
                value_ref[r, w : w + TILE, lanes] = (
                    value * sig * (1.0 + gate * (1.0 - sig))
                ).astype(BF16)
                mixed.append((value * gated).astype(BF16))
            tokens = pl.ds(pl.multiple_of(r * across, LANES), across)
            mixed_ref[lanes, tokens] = jnp.concatenate(mixed, axis=0).T


def conv_parts(hidden, weights):
    _, height, across, channels = hidden.shape
    size = height * across * channels
    return pl.pallas_call(
        conv_kernel,
        in_specs=[VMEM, VMEM],
        out_specs=[VMEM] * 3,
        out_shape=[
            jax.ShapeDtypeStruct((height, across, channels), BF16),
            jax.ShapeDtypeStruct((height, across, channels), BF16),
            jax.ShapeDtypeStruct((channels, height * across), BF16),
        ],
        scratch_shapes=[pltpu.VMEM((2, height + 2, across + 2 * PAD, LANES), F32)],
        compiler_params=params(),
        cost_estimate=cost(size * 60, size * 14, size),
    )(hidden, weights)


def gather_rows(n, place_ref, pieces, full_ref):
    across = pieces[0].shape[0]
    spot = ring_place(place_ref[0], n)
    starts = [at_ring(spot, n) * across]
    for step in range(1, n // 2):
        starts.append(at_ring(spot - step, n) * across)
        starts.append(at_ring(spot + step, n) * across)
    far = at_ring(spot + n // 2, n) * across
    starts.extend([far, far + across // 2])
    for piece, start in zip(pieces, starts):
        rows = piece.shape[0]
        full_ref[pl.ds(pl.multiple_of(start, rows), rows)] = piece[...]


def column_sums(place_ref, mixed_ref, full_ref, send_ref, keep_ref):
    core = place_ref[1]
    half = full_ref.shape[1] // 2
    for out_ref, column in ((send_ref, 1 - core), (keep_ref, core)):
        columns = pl.ds(pl.multiple_of(column * half, LANES), half)
        out_ref[...] = jnp.dot(
            mixed_ref[...], full_ref[:, columns], preferred_element_type=F32
        ).astype(out_ref.dtype)


def row_products(offset, full_ref, weight_ref, before_ref, grad_ref):
    tokens, width = full_ref.shape
    slab = min(tokens, 512)

    @pl.loop(0, tokens // slab)
    def _(s):
        rows = pl.ds(pl.multiple_of(s * slab, slab), slab)
        grad = lax.dot_general(
            full_ref[rows],
            weight_ref[:, offset : offset + width],
            (((1,), (1,)), ((), ())),
            preferred_element_type=F32,
        )
        if before_ref is not None:
            grad = grad + before_ref[rows]
        grad_ref[rows] = grad


def chunk_kernel(n, offset, product, added, place_ref, *refs):
    pieces, refs = refs[: n + 1], refs[n + 1 :]
    full_ref = refs[-1]
    gather_rows(n, place_ref, pieces, full_ref)
    if not product:
        mixed_ref, send_ref, keep_ref = refs[:3]
    elif added:
        mixed_ref, weight_ref, before_ref, send_ref, keep_ref, grad_ref = refs[:6]
    else:
        mixed_ref, weight_ref, send_ref, keep_ref, grad_ref = refs[:5]
        before_ref = None
    column_sums(place_ref, mixed_ref, full_ref, send_ref, keep_ref)
    if product:
        row_products(offset, full_ref, weight_ref, before_ref, grad_ref)


def chunk_parts(n, place, pieces, offset, mixed, weight=None, before=None):
    across, width = pieces[0].shape
    channels, tokens = mixed.shape
    product, added = weight is not None, before is not None
    operands = [*pieces, mixed] + [v for v in (weight, before) if v is not None]
    out_shape = [
        jax.ShapeDtypeStruct((channels, width // 2), BF16),
        jax.ShapeDtypeStruct((channels, width // 2), F32),
    ]
    if product:
        out_shape.append(jax.ShapeDtypeStruct((tokens, channels), F32))
    return pl.pallas_call(
        functools.partial(chunk_kernel, n, offset, product, added),
        in_specs=[SMEM] + [VMEM] * len(operands),
        out_specs=[VMEM] * len(out_shape),
        out_shape=out_shape,
        scratch_shapes=[pltpu.VMEM((tokens, width), BF16)],
        compiler_params=params(),
        cost_estimate=cost(
            2 * (1 + product) * tokens * channels * width,
            tokens * width * 2 + channels * width * 5 + tokens * channels * 10,
        ),
    )(place, *operands)


def grads_kernel(n, offset, place_ref, *refs):
    pieces, refs = refs[: n + 1], refs[n + 1 :]
    weight_ref, before_ref, gate_ref, value_ref, hidden_ref, taps_ref = refs[:6]
    out_ref, term_ref, full_ref, grad_ref, pad_ref = refs[6:]
    _, height, across, channels = hidden_ref.shape
    gather_rows(n, place_ref, pieces, full_ref)
    row_products(offset, full_ref, weight_ref, before_ref, grad_ref)
    clear_edges(pad_ref, height, across)

    @pl.loop(0, channels // LANES)
    def _(c):
        lanes = pl.ds(pl.multiple_of(c * LANES, LANES), LANES)

        @pl.loop(0, height)
        def _(r):
            grad = grad_ref[pl.ds(pl.multiple_of(r * across, across), across), lanes]
            for k, factor in enumerate((gate_ref, value_ref)):
                pad_ref[k, r + 1, PAD : PAD + across] = grad * factor[r, :, lanes].astype(F32)

        weights = taps_ref[:, lanes]
        for k in range(2):

            def row(r, sums):
                sums = list(sums)
                for t in range(across // TILE):
                    w = t * TILE
                    own = hidden_ref[k, r, w : w + TILE, lanes].astype(F32)
                    total = None
                    for i in range(3):
                        for j in range(3):
                            view = pad_ref[k, r + 2 - i, PAD + w + 1 - j : PAD + w + 1 - j + TILE]
                            term = weights[(i * 3 + j) * 2 + k][None, :] * view
                            total = term if total is None else total + term
                            both = view * own
                            sums[i * 3 + j] = sums[i * 3 + j] + (both[:8] + both[8:])
                    out_ref[k, r, w : w + TILE, lanes] = total.astype(BF16)
                return tuple(sums)

            sums = lax.fori_loop(0, height, row, tuple(jnp.zeros((8, LANES), F32) for _ in range(9)))
            for tap in range(9):
                term_ref[tap * 2 + k : tap * 2 + k + 1, lanes] = jnp.sum(
                    sums[tap], axis=0, keepdims=True
                )


def grads(n, place, pieces, offset, weight, before, gate_part, value_part, hidden, taps):
    _, height, across, channels = hidden.shape
    width = pieces[0].shape[1]
    tokens = height * across
    size = tokens * channels
    operands = [*pieces, weight, before, gate_part, value_part, hidden, taps]
    return pl.pallas_call(
        functools.partial(grads_kernel, n, offset),
        in_specs=[SMEM] + [VMEM] * len(operands),
        out_specs=[VMEM, VMEM],
        out_shape=[
            jax.ShapeDtypeStruct(hidden.shape, BF16),
            jax.ShapeDtypeStruct((18, channels), F32),
        ],
        scratch_shapes=[
            pltpu.VMEM((tokens, width), BF16),
            pltpu.VMEM((tokens, channels), F32),
            pltpu.VMEM((2, height + 2, across + 2 * PAD, LANES), F32),
        ],
        compiler_params=params(),
        cost_estimate=cost(size * 80, size * 20),
    )(place, *operands)


def put_kernel(offset, place_ref, mine_ref, other_ref, *refs):
    out_ref, sems = refs[-2:]
    half = mine_ref.shape[1]
    copies = []
    for slot, (ref, column) in enumerate(((mine_ref, place_ref[1]), (other_ref, 1 - place_ref[1]))):
        columns = pl.ds(pl.multiple_of(offset + column * half, LANES), half)
        copies.append(pltpu.make_async_copy(ref, out_ref.at[:, columns], sems.at[slot]))
    for copy in copies:
        copy.start()
    for copy in copies:
        copy.wait()


def put(place, mine, other, whole, offset, shape):
    hbm = pl.BlockSpec(memory_space=pl.ANY)
    arrays = [mine, other] + ([] if whole is None else [whole])
    return pl.pallas_call(
        functools.partial(put_kernel, offset),
        in_specs=[SMEM] + [hbm] * len(arrays),
        out_specs=hbm,
        out_shape=jax.ShapeDtypeStruct(shape, BF16),
        scratch_shapes=[pltpu.SemaphoreType.DMA((2,))],
        input_output_aliases={} if whole is None else {3: 0},
        compiler_params=params(),
        cost_estimate=cost(0, mine.size * 8),
    )(place, *arrays)


class Ring:
    def __init__(self, n):
        ring = ring_order(n)
        self.right = [(ring[i], ring[(i + 1) % n]) for i in range(n)]
        self.left = [(ring[i], ring[(i - 1) % n]) for i in range(n)]
        self.last = n // 2
        self.stage = 0

    def begin(self, own):
        self.edge = [own, own]
        self.pieces = [own]

    def step(self):
        self.stage += 1
        up, down = self.edge
        if self.stage == self.last:
            half = up.shape[0] // 2
            up, down = up[:half], down[half:]
        up = lax.ppermute(up, "tensor", self.right)
        down = lax.ppermute(down, "tensor", self.left)
        self.edge = [up, down]
        self.pieces += [up, down]


class Order:
    def __init__(self, token):
        self.token = token

    def after(self, values, waited):
        flat, tree = jax.tree.flatten((values, waited, self.token))
        values, _, self.token = jax.tree.unflatten(tree, lax.optimization_barrier(flat))
        return values


def swap(value, bit):
    n = lax.axis_size("dp")
    return lax.ppermute(value, "dp", [(i, i ^ bit) for i in range(n)])


def sum_rest(value, low=2):
    bit = low
    while bit < lax.axis_size("dp"):
        value = value.astype(F32) + swap(value, bit).astype(F32)
        if bit * 2 < lax.axis_size("dp"):
            value = value.astype(BF16)
        bit *= 2
    return value


def on_device(hidden_in, conv_weight, proj_weight, out_grad, sample_gate):
    samples, height, across, _, channels = hidden_in.shape
    depth = out_grad.shape[-1]
    n = lax.axis_size("tensor")
    dp = lax.axis_size("dp")
    assert samples == 1 and out_grad.shape[1] == 1 and n % 2 == 0 and dp & (dp - 1) == 0
    grad_scale = 1.0 / math.sqrt(dp * samples * height * across)
    place = jnp.stack([lax.axis_index("tensor"), lax.rem(lax.axis_index("dp"), 2)]).astype(
        jnp.int32
    )
    own = out_grad.reshape(across, depth)
    hidden = jnp.transpose(hidden_in.reshape(height, across, 2, channels), (2, 0, 1, 3))
    taps = conv_weight.astype(F32).reshape(18, channels)

    widths = split_widths(depth)
    offsets = [sum(widths[:k]) for k in range(len(widths))]
    first, second = Ring(n), Ring(n)
    last = n // 2
    order = Order(place)

    def block(k):
        columns = slice(offsets[k], offsets[k] + widths[k])
        return (own[:, columns].astype(F32) * sample_gate[:, columns]).astype(BF16)

    def move(ring, waited=()):
        ring.edge = order.after(ring.edge, waited)
        ring.step()

    first.begin(block(0))
    first.step()
    hidden, source = order.after((hidden, block(1)), ())
    second.begin(source)
    move(first, (first.edge, hidden))
    hidden = order.after(hidden, ())
    conv = conv_parts(hidden, taps)
    for step in range(3, last + 1):
        move(second, (second.edge, conv))
        move(first, first.edge)
    move(second, second.edge)
    pieces = order.after(first.pieces, first.edge)
    send, keep, grad = chunk_parts(n, order.token, pieces, offsets[0], conv[2], proj_weight)
    if second.stage < last:
        second.edge = order.after(second.edge, (second.edge, grad))
        second.step()
    send = order.after(send, grad)
    pair0 = (keep + swap(send, 1).astype(F32)).astype(BF16)
    pair0 = order.after(pair0, ())
    units = 2
    unit = pair0.shape[1] // units
    sums0 = [sum_rest(pair0[:, u * unit : (u + 1) * unit]) for u in range(units)]

    pieces = order.after(second.pieces, second.edge)
    gate_part, value_part, mixed = conv
    send, keep = chunk_parts(n, order.token, pieces, offsets[1], mixed)
    send = order.after(send, keep)
    pair1 = (keep + swap(send, 1).astype(F32)).astype(BF16)
    pair1 = order.after(pair1, sums0[0])
    sums1 = [sum_rest(pair1[:, u * unit : (u + 1) * unit]) for u in range(units)]
    grad = order.after(grad, ())
    hidden_grad, terms = grads(
        n,
        order.token,
        pieces,
        offsets[1],
        proj_weight,
        grad,
        gate_part,
        value_part,
        hidden,
        taps,
    )
    total = order.after(terms, ())
    bit = 1
    while bit < dp:
        total = total + swap(total, bit)
        bit *= 2
    conv_grad = (total * grad_scale).reshape(3, 3, 2, channels)
    hidden_grad = jnp.transpose(hidden_grad, (1, 2, 0, 3))[None]
    whole = None
    for k, sums in ((0, sums0), (1, sums1)):
        mine = (jnp.concatenate(sums, axis=1) * grad_scale).astype(BF16)
        mine = order.after(mine, ())
        whole = put(order.token, mine, swap(mine, 1), whole, offsets[k], (channels, depth))
    return (hidden_grad, whole, conv_grad)


def solution(mesh):
    in_specs = (
        P("dp", None, None, None, "tensor"),
        P(None, None, None, "tensor"),
        P("tensor", None),
        P("dp", "tensor", None, None),
        P("dp", None),
    )
    out_specs = (
        P("dp", None, None, None, "tensor"),
        P("tensor", None),
        P(None, None, None, "tensor"),
    )
    return jax.shard_map(
        on_device, mesh=mesh, in_specs=in_specs, out_specs=out_specs, check_vma=False
    )
```

```python
import functools
import math

import jax
import jax.numpy as jnp
from jax import lax
from jax.experimental import pallas as pl
from jax.experimental.layout import Layout, with_layout_constraint
from jax.experimental.pallas import tpu as pltpu
from jax.sharding import PartitionSpec as P

F32 = jnp.float32
BF16 = jnp.bfloat16
PAD = 8
TILE = 16
LANES = 128
VMEM_BYTES = 20 * 1024 * 1024
VMEM = pl.BlockSpec(memory_space=pltpu.VMEM)
SMEM = pl.BlockSpec(memory_space=pltpu.SMEM)


def ring_order(n):
    return [2 * i if i < n // 2 else 2 * (n - 1 - i) + 1 for i in range(n)]


def at_ring(position, n):
    position = lax.rem(position + 2 * n, n)
    return jnp.where(position < n // 2, 2 * position, 2 * (n - 1 - position) + 1)


def ring_place(index, n):
    half = index // 2
    return jnp.where(lax.rem(index, 2) == 0, half, n - 1 - half)


def params(limit=VMEM_BYTES):
    return pltpu.CompilerParams(vmem_limit_bytes=limit)


def cost(flops, moved, transcendentals=0):
    return pl.CostEstimate(flops=1, bytes_accessed=1, transcendentals=0)


def clear_edges(pad_ref, height, across):
    lanes = pad_ref.shape[-1]
    for k in range(2):
        pad_ref[k, 0] = jnp.zeros(pad_ref.shape[2:], F32)
        pad_ref[k, height + 1] = jnp.zeros(pad_ref.shape[2:], F32)

        @pl.loop(0, height)
        def _(r):
            pad_ref[k, r + 1, 0:PAD] = jnp.zeros((PAD, lanes), F32)
            pad_ref[k, r + 1, PAD + across : 2 * PAD + across] = jnp.zeros((PAD, lanes), F32)


def conv_kernel(hidden_ref, weight_ref, gate_ref, value_ref, mixed_ref, pad_ref):
    _, height, across, channels = hidden_ref.shape
    clear_edges(pad_ref, height, across)

    @pl.loop(0, channels // LANES)
    def _(c):
        lanes = pl.ds(pl.multiple_of(c * LANES, LANES), LANES)

        @pl.loop(0, height)
        def _(r):
            for k in range(2):
                pad_ref[k, r + 1, PAD : PAD + across] = hidden_ref[k, r, :, lanes].astype(F32)

        weights = weight_ref[:, lanes]

        @pl.loop(0, height)
        def _(r):
            mixed = []
            for t in range(across // TILE):
                w = t * TILE
                parts = []
                for k in range(2):
                    total = None
                    for i in range(3):
                        for j in range(3):
                            view = pad_ref[k, r + i, PAD + w + j - 1 : PAD + w + j - 1 + TILE]
                            term = weights[(i * 3 + j) * 2 + k][None, :] * view
                            total = term if total is None else total + term
                    parts.append(total)
                value, gate = parts
                sig = 1.0 / (1.0 + jnp.exp(-gate))
                gated = gate * sig
                gate_ref[r, w : w + TILE, lanes] = gated.astype(BF16)
                value_ref[r, w : w + TILE, lanes] = (
                    value * sig * (1.0 + gate * (1.0 - sig))
                ).astype(BF16)
                mixed.append((value * gated).astype(BF16))
            tokens = pl.ds(pl.multiple_of(r * across, LANES), across)
            mixed_ref[lanes, tokens] = jnp.concatenate(mixed, axis=0).T


def conv_parts(hidden, weights):
    _, height, across, channels = hidden.shape
    size = height * across * channels
    return pl.pallas_call(
        conv_kernel,
        in_specs=[VMEM, VMEM],
        out_specs=[VMEM] * 3,
        out_shape=[
            jax.ShapeDtypeStruct((height, across, channels), BF16),
            jax.ShapeDtypeStruct((height, across, channels), BF16),
            jax.ShapeDtypeStruct((channels, height * across), BF16),
        ],
        scratch_shapes=[pltpu.VMEM((2, height + 2, across + 2 * PAD, LANES), F32)],
        compiler_params=params(),
        cost_estimate=cost(size * 60, size * 14, size),
    )(hidden, weights)


def rows_kernel(n, numbers, far, added, place_ref, *refs):
    count = len(numbers)
    pieces, refs = refs[: count + far], refs[count + far :]
    gate_ref, weight_ref, mixed_ref = refs[:3]
    sums_ref, grad_ref, local_ref, side_ref = refs[-4:]
    before_ref = refs[3] if added else None
    across = local_ref.shape[0] // count
    depth = local_ref.shape[1]
    spot = ring_place(place_ref[0], n)
    starts = [
        pl.multiple_of(at_ring(spot + (0 if p == 0 else (p // 2 if p % 2 == 0 else -(p + 1) // 2)), n) * across, LANES)
        for p in numbers
    ]
    base = 0
    for piece in pieces:
        for r in range(0, piece.shape[0], TILE):
            local_ref[base + r : base + r + TILE] = (
                piece[r : r + TILE].astype(F32) * gate_ref[...]
            ).astype(BF16)
        base += piece.shape[0]
    for k, start in enumerate(starts):
        side_ref[:, k * across : (k + 1) * across] = mixed_ref[:, pl.ds(start, across)]
    block = min(depth, 512)
    for c in range(0, depth, block):
        total = jnp.dot(
            side_ref[...], local_ref[:, c : c + block], preferred_element_type=F32
        )
        if added:
            total = total + before_ref[:, c : c + block]
        sums_ref[:, c : c + block] = total
    product = lax.dot_general(
        local_ref[...], weight_ref[...], (((1,), (1,)), ((), ())), preferred_element_type=F32
    )
    for k, start in enumerate(starts):
        grad_ref[pl.ds(start, across)] = product[k * across : (k + 1) * across]


def rows_parts(n, place, pieces, numbers, far, gate, weight, mixed, before=None):
    depth = pieces[0].shape[1]
    channels, tokens = mixed.shape
    count, across = len(numbers), tokens // n
    operands = [*pieces, gate, weight, mixed]
    aliases = {}
    if before is not None:
        aliases = {len(operands) + 1: 0, len(operands) + 2: 1}
        operands += before
    return pl.pallas_call(
        functools.partial(rows_kernel, n, numbers, far, before is not None),
        in_specs=[SMEM] + [VMEM] * len(operands),
        out_specs=[VMEM] * 2,
        out_shape=[
            jax.ShapeDtypeStruct((channels, depth), F32),
            jax.ShapeDtypeStruct((tokens, channels), F32),
        ],
        scratch_shapes=[
            pltpu.VMEM((count * across, depth), BF16),
            pltpu.VMEM((channels, count * across), BF16),
        ],
        input_output_aliases=aliases,
        compiler_params=params(),
        cost_estimate=cost(4 * count * across * channels * depth, 0),
    )(place, *operands)


def far_kernel(n, first, place_ref, up_ref, down_ref, gate_ref, mixed_ref, before_ref, *refs):
    send_ref, keep_ref, local_ref = refs
    half = up_ref.shape[0]
    across = 2 * half
    width = send_ref.shape[1]
    core = place_ref[1]
    start = pl.multiple_of(at_ring(ring_place(place_ref[0], n) + n // 2, n) * across, LANES)
    columns = pl.ds(first, 2 * width)
    for base, piece in ((0, up_ref), (half, down_ref)):
        for r in range(0, half, TILE):
            local_ref[base + r : base + r + TILE] = (
                piece[r : r + TILE, columns].astype(F32) * gate_ref[:, columns]
            ).astype(BF16)
    for out_ref, side in ((send_ref, 1 - core), (keep_ref, core)):
        column = side * width
        total = jnp.dot(
            mixed_ref[:, pl.ds(start, across)],
            local_ref[:, pl.ds(pl.multiple_of(column, LANES), width)],
            preferred_element_type=F32,
        )
        total = total + before_ref[:, pl.ds(pl.multiple_of(first + column, LANES), width)]
        out_ref[...] = total.astype(out_ref.dtype)


def far_parts(n, place, pieces, first, width, gate, mixed, before):
    channels, tokens = mixed.shape
    return pl.pallas_call(
        functools.partial(far_kernel, n, first),
        in_specs=[SMEM] + [VMEM] * 5,
        out_specs=[VMEM] * 2,
        out_shape=[
            jax.ShapeDtypeStruct((channels, width), BF16),
            jax.ShapeDtypeStruct((channels, width), F32),
        ],
        scratch_shapes=[pltpu.VMEM((tokens // n, 2 * width), BF16)],
        compiler_params=params(),
        cost_estimate=cost(1, 1),
    )(place, *pieces, gate, mixed, before)


def far_row_kernel(n, place_ref, up_ref, down_ref, gate_ref, weight_ref, before_ref, grad_ref, local_ref):
    half = up_ref.shape[0]
    across = 2 * half
    start = pl.multiple_of(at_ring(ring_place(place_ref[0], n) + n // 2, n) * across, LANES)
    for base, piece in ((0, up_ref), (half, down_ref)):
        for r in range(0, half, TILE):
            local_ref[base + r : base + r + TILE] = (
                piece[r : r + TILE].astype(F32) * gate_ref[...]
            ).astype(BF16)
    grad_ref[pl.ds(start, across)] = lax.dot_general(
        local_ref[...], weight_ref[...], (((1,), (1,)), ((), ())), preferred_element_type=F32
    )


def far_row(n, place, pieces, gate, weight, before):
    tokens, channels = before.shape
    return pl.pallas_call(
        functools.partial(far_row_kernel, n),
        in_specs=[SMEM] + [VMEM] * 5,
        out_specs=VMEM,
        out_shape=jax.ShapeDtypeStruct(before.shape, F32),
        scratch_shapes=[pltpu.VMEM((tokens // n, weight.shape[1]), BF16)],
        input_output_aliases={5: 0},
        compiler_params=params(),
        cost_estimate=cost(1, 1),
    )(place, *pieces, gate, weight, before)


def grads_kernel(
    grad_ref, gate_ref, value_ref, hidden_ref, taps_ref, out_ref, term_ref, pad_ref
):
    _, height, across, channels = hidden_ref.shape
    clear_edges(pad_ref, height, across)

    @pl.loop(0, channels // LANES)
    def _(c):
        lanes = pl.ds(pl.multiple_of(c * LANES, LANES), LANES)

        @pl.loop(0, height)
        def _(r):
            grad = grad_ref[pl.ds(pl.multiple_of(r * across, across), across), lanes]
            for k, factor in enumerate((gate_ref, value_ref)):
                pad_ref[k, r + 1, PAD : PAD + across] = grad * factor[r, :, lanes].astype(F32)

        weights = taps_ref[:, lanes]
        for k in range(2):

            def row(r, sums):
                sums = list(sums)
                for t in range(across // TILE):
                    w = t * TILE
                    own = hidden_ref[k, r, w : w + TILE, lanes].astype(F32)
                    total = None
                    for i in range(3):
                        for j in range(3):
                            view = pad_ref[k, r + 2 - i, PAD + w + 1 - j : PAD + w + 1 - j + TILE]
                            term = weights[(i * 3 + j) * 2 + k][None, :] * view
                            total = term if total is None else total + term
                            both = view * own
                            sums[i * 3 + j] = sums[i * 3 + j] + (both[:8] + both[8:])
                    out_ref[k, r, w : w + TILE, lanes] = total.astype(BF16)
                return tuple(sums)

            sums = lax.fori_loop(0, height, row, tuple(jnp.zeros((8, LANES), F32) for _ in range(9)))
            for tap in range(9):
                term_ref[tap // 3, tap % 3, k : k + 1, lanes] = jnp.sum(
                    sums[tap], axis=0, keepdims=True
                )


def grads(grad, gate_part, value_part, hidden, taps):
    _, height, across, channels = hidden.shape
    size = height * across * channels
    return pl.pallas_call(
        grads_kernel,
        in_specs=[VMEM] * 5,
        out_specs=[VMEM, VMEM],
        out_shape=[
            jax.ShapeDtypeStruct(hidden.shape, BF16),
            jax.ShapeDtypeStruct((3, 3, 2, channels), F32),
        ],
        scratch_shapes=[pltpu.VMEM((2, height + 2, across + 2 * PAD, LANES), F32)],
        compiler_params=params(),
        cost_estimate=cost(size * 80, size * 20),
    )(grad, gate_part, value_part, hidden, taps)


def put_kernel(firsts, place_ref, *refs):
    count = len(firsts)
    out_ref, sems = refs[-2:]
    copies = []
    for u, first in enumerate(firsts):
        for k, core in ((u, place_ref[1]), (count + u, 1 - place_ref[1])):
            half = refs[k].shape[1]
            columns = pl.ds(pl.multiple_of(first + core * half, LANES), half)
            copies.append(
                pltpu.make_async_copy(refs[k], out_ref.at[:, columns], sems.at[k])
            )
    for copy in copies:
        copy.start()
    for copy in copies:
        copy.wait()


def put(place, mines, others, firsts, whole, shape):
    hbm = pl.BlockSpec(memory_space=pl.ANY)
    arrays = [*mines, *others] + ([] if whole is None else [whole])
    return pl.pallas_call(
        functools.partial(put_kernel, firsts),
        in_specs=[SMEM] + [hbm] * len(arrays),
        out_specs=hbm,
        out_shape=jax.ShapeDtypeStruct(shape, BF16),
        scratch_shapes=[pltpu.SemaphoreType.DMA((2 * len(mines),))],
        input_output_aliases={} if whole is None else {len(arrays): 0},
        compiler_params=params(),
        cost_estimate=cost(1, 1),
    )(place, *arrays)


class Order:
    def __init__(self, token):
        self.token = token

    def after(self, values, waited):
        flat, tree = jax.tree.flatten((values, waited, self.token))
        values, _, self.token = jax.tree.unflatten(tree, lax.optimization_barrier(flat))
        return values


def swap(value, bit):
    n = lax.axis_size("dp")
    return lax.ppermute(value, "dp", [(i, i ^ bit) for i in range(n)])


def sum_far(value, received):
    dp = lax.axis_size("dp")
    value = value.astype(F32) + received.astype(F32)
    bit = 4
    while bit < dp:
        value = value.astype(BF16)
        value = value.astype(F32) + swap(value, bit).astype(F32)
        bit *= 2
    return value


def sum_groups(value):
    dp = lax.axis_size("dp")
    bit = 1
    if dp >= 4:
        one, two, three = swap(value, 1), swap(value, 2), swap(value, 3)
        value = (value + one) + (two + three)
        bit = 4
    while bit < dp:
        value = value + swap(value, bit)
        bit *= 2
    return value


def on_device(hidden_in, conv_weight, proj_weight, out_grad, sample_gate):
    samples, height, across, _, channels = hidden_in.shape
    depth = out_grad.shape[-1]
    n = lax.axis_size("tensor")
    dp = lax.axis_size("dp")
    assert samples == 1 and out_grad.shape[1] == 1 and n % 2 == 0
    assert dp >= 4 and dp & (dp - 1) == 0
    grad_scale = 1.0 / math.sqrt(dp * samples * height * across)
    place = jnp.stack([lax.axis_index("tensor"), lax.rem(lax.axis_index("dp"), 2)]).astype(
        jnp.int32
    )
    own = out_grad.reshape(across, depth)
    hidden = jnp.transpose(hidden_in.reshape(height, across, 2, channels), (2, 0, 1, 3))
    taps = conv_weight.astype(F32).reshape(18, channels)
    order = Order(place)
    ring = ring_order(n)
    right = [(ring[i], ring[(i + 1) % n]) for i in range(n)]
    left = [(ring[i], ring[(i - 1) % n]) for i in range(n)]
    last = n // 2

    def rows(pieces, numbers, before):
        return rows_parts(n, order.token, pieces, numbers, 0, sample_gate, proj_weight, mixed, before)

    up = down = own
    pieces, numbers, before = [own], [0], None
    for stage in range(1, last + 1):
        if stage > 1:
            up = order.after(up, ())
        arrived = [up]
        up = lax.ppermute(up if stage < last else up[: across // 2], "tensor", right)
        if stage > 1:
            down = order.after(down, ())
        arrived.append(down)
        down = lax.ppermute(down if stage < last else down[across // 2 :], "tensor", left)
        if stage > 1:
            pieces += arrived
            numbers += [2 * stage - 3, 2 * stage - 2]
        if stage == 1:
            hidden = order.after(hidden, ())
            gate_part, value_part, mixed = conv_parts(hidden, taps)
            gate_part, value_part, mixed = order.after((gate_part, value_part, mixed), ())
        elif stage > 2:
            before = order.after(rows(pieces, numbers, before), ())
            pieces, numbers = [], []
    up, down = order.after((up, down), ())
    assert not pieces
    sums, grad = before
    far = [up, down]

    eighth = depth // 8
    widths = [eighth, 3 * eighth // 2, 3 * eighth // 2]
    firsts = [0, 2 * eighth, 5 * eighth]
    near, keeps, pairs, far_sums, mines, others = [], [], [], [], [], []
    for first, width in zip(firsts, widths):
        (send, keep) = far_parts(n, order.token, far, first, width, sample_gate, mixed, sums)
        (send, keep, sums) = order.after((send, keep, sums), ())
        near.append(swap(send, 1))
        keeps.append(keep)

    def begin(u):
        received = order.after(near[u], ())
        pairs.append(order.after((keeps[u] + received.astype(F32)).astype(BF16), ()))
        far_sums.append(swap(pairs[u], 2))

    def finish(u):
        received = order.after(far_sums[u], ())
        mine = (sum_far(pairs[u], received) * grad_scale).astype(BF16)
        mines.append(order.after(mine, ()))
        others.append(swap(mines[u], 1))

    begin(0)
    begin(1)
    begin(2)
    grad = order.after(grad, ())
    grad = far_row(n, order.token, far, sample_gate, proj_weight, grad)
    hidden_grad, terms = grads(grad, gate_part, value_part, hidden, taps)
    terms, hidden_grad = order.after((terms, hidden_grad), ())
    total = sum_groups(terms)
    finish(0)
    hidden_grad = with_layout_constraint(
        jnp.transpose(hidden_grad, (1, 2, 0, 3)), Layout(major_to_minor=(0, 1, 2, 3))
    )
    hidden_grad = order.after(hidden_grad, ())
    finish(1)
    total, far_sums[2] = order.after((total, far_sums[2]), ())
    conv_grad = total * grad_scale
    others[0] = order.after(others[0], ())
    others[1] = order.after(others[1], ())
    finish(2)
    shape = (channels, depth)
    whole = put(order.token, mines[:2], others[:2], firsts[:2], None, shape)
    conv_grad = order.after(conv_grad, whole)
    others[2] = order.after(others[2], ())
    whole = put(order.token, mines[2:], others[2:], firsts[2:], whole, shape)
    return (hidden_grad[None], whole, conv_grad)


def solution(mesh):
    in_specs = (
        P("dp", None, None, None, "tensor"),
        P(None, None, None, "tensor"),
        P("tensor", None),
        P("dp", "tensor", None, None),
        P("dp", None),
    )
    out_specs = (
        P("dp", None, None, None, "tensor"),
        P("tensor", None),
        P(None, None, None, "tensor"),
    )
    return jax.shard_map(
        on_device, mesh=mesh, in_specs=in_specs, out_specs=out_specs, check_vma=False
    )
```

```python
import functools
import math

import jax
import jax.numpy as jnp
from jax import lax
from jax.experimental import pallas as pl
from jax.experimental.layout import Layout, with_layout_constraint
from jax.experimental.pallas import tpu as pltpu
from jax.sharding import PartitionSpec as P

F32 = jnp.float32
BF16 = jnp.bfloat16
PAD = 8
TILE = 16
LANES = 128
VMEM_BYTES = 20 * 1024 * 1024
VMEM = pl.BlockSpec(memory_space=pltpu.VMEM)
SMEM = pl.BlockSpec(memory_space=pltpu.SMEM)


def ring_order(n):
    return [2 * i if i < n // 2 else 2 * (n - 1 - i) + 1 for i in range(n)]


def at_ring(position, n):
    position = lax.rem(position + 2 * n, n)
    return jnp.where(position < n // 2, 2 * position, 2 * (n - 1 - position) + 1)


def ring_place(index, n):
    half = index // 2
    return jnp.where(lax.rem(index, 2) == 0, half, n - 1 - half)


def params(limit=VMEM_BYTES):
    return pltpu.CompilerParams(vmem_limit_bytes=limit)


def cost(flops, moved, transcendentals=0):
    return pl.CostEstimate(flops=1, bytes_accessed=1, transcendentals=0)


def clear_edges(pad_ref, height, across):
    lanes = pad_ref.shape[-1]
    for k in range(2):
        pad_ref[k, 0] = jnp.zeros(pad_ref.shape[2:], F32)
        pad_ref[k, height + 1] = jnp.zeros(pad_ref.shape[2:], F32)

        @pl.loop(0, height)
        def _(r):
            pad_ref[k, r + 1, 0:PAD] = jnp.zeros((PAD, lanes), F32)
            pad_ref[k, r + 1, PAD + across : 2 * PAD + across] = jnp.zeros((PAD, lanes), F32)


def conv_kernel(hidden_ref, weight_ref, gate_ref, value_ref, mixed_ref, pad_ref):
    _, height, across, channels = hidden_ref.shape
    clear_edges(pad_ref, height, across)

    @pl.loop(0, channels // LANES)
    def _(c):
        lanes = pl.ds(pl.multiple_of(c * LANES, LANES), LANES)

        @pl.loop(0, height)
        def _(r):
            for k in range(2):
                pad_ref[k, r + 1, PAD : PAD + across] = hidden_ref[k, r, :, lanes].astype(F32)

        weights = weight_ref[:, lanes]

        @pl.loop(0, height)
        def _(r):
            mixed = []
            for t in range(across // TILE):
                w = t * TILE
                parts = []
                for k in range(2):
                    total = None
                    for i in range(3):
                        for j in range(3):
                            view = pad_ref[k, r + i, PAD + w + j - 1 : PAD + w + j - 1 + TILE]
                            term = weights[(i * 3 + j) * 2 + k][None, :] * view
                            total = term if total is None else total + term
                    parts.append(total)
                value, gate = parts
                sig = 1.0 / (1.0 + jnp.exp(-gate))
                gated = gate * sig
                gate_ref[r, w : w + TILE, lanes] = gated.astype(BF16)
                value_ref[r, w : w + TILE, lanes] = (
                    value * sig * (1.0 + gate * (1.0 - sig))
                ).astype(BF16)
                mixed.append((value * gated).astype(BF16))
            tokens = pl.ds(pl.multiple_of(r * across, LANES), across)
            mixed_ref[lanes, tokens] = jnp.concatenate(mixed, axis=0).T


def conv_parts(hidden, weights):
    _, height, across, channels = hidden.shape
    size = height * across * channels
    return pl.pallas_call(
        conv_kernel,
        in_specs=[VMEM, VMEM],
        out_specs=[VMEM] * 3,
        out_shape=[
            jax.ShapeDtypeStruct((height, across, channels), BF16),
            jax.ShapeDtypeStruct((height, across, channels), BF16),
            jax.ShapeDtypeStruct((channels, height * across), BF16),
        ],
        scratch_shapes=[pltpu.VMEM((2, height + 2, across + 2 * PAD, LANES), F32)],
        compiler_params=params(),
        cost_estimate=cost(size * 60, size * 14, size),
    )(hidden, weights)


def rows_kernel(n, parts, numbers, added, place_ref, *refs):
    count = len(numbers)
    pieces, refs = refs[:parts], refs[parts:]
    gate_ref, weight_ref, mixed_ref = refs[:3]
    sums_ref, grad_ref, local_ref, side_ref = refs[-4:]
    before_ref = refs[3] if added else None
    across = local_ref.shape[0] // count
    depth = local_ref.shape[1]
    spot = ring_place(place_ref[0], n)
    starts = [
        pl.multiple_of(at_ring(spot + step, n) * across, LANES) for step in numbers
    ]
    base = 0
    for piece in pieces:
        for r in range(0, piece.shape[0], TILE):
            local_ref[base + r : base + r + TILE] = (
                piece[r : r + TILE].astype(F32) * gate_ref[...]
            ).astype(BF16)
        base += piece.shape[0]
    for k, start in enumerate(starts):
        side_ref[:, k * across : (k + 1) * across] = mixed_ref[:, pl.ds(start, across)]
    block = min(depth, 512)
    for c in range(0, depth, block):
        total = jnp.dot(
            side_ref[...], local_ref[:, c : c + block], preferred_element_type=F32
        )
        if added:
            total = total + before_ref[:, c : c + block]
        sums_ref[:, c : c + block] = total
    product = lax.dot_general(
        local_ref[...], weight_ref[...], (((1,), (1,)), ((), ())), preferred_element_type=F32
    )
    for k, start in enumerate(starts):
        grad_ref[pl.ds(start, across)] = product[k * across : (k + 1) * across]


def rows_parts(n, place, pieces, numbers, gate, weight, mixed, before=None):
    depth = pieces[0].shape[1]
    channels, tokens = mixed.shape
    count, across = len(numbers), tokens // n
    operands = [*pieces, gate, weight, mixed]
    aliases = {}
    if before is not None:
        aliases = {len(operands) + 1: 0, len(operands) + 2: 1}
        operands += before
    return pl.pallas_call(
        functools.partial(rows_kernel, n, len(pieces), numbers, before is not None),
        in_specs=[SMEM] + [VMEM] * len(operands),
        out_specs=[VMEM] * 2,
        out_shape=[
            jax.ShapeDtypeStruct((channels, depth), F32),
            jax.ShapeDtypeStruct((tokens, channels), F32),
        ],
        scratch_shapes=[
            pltpu.VMEM((count * across, depth), BF16),
            pltpu.VMEM((channels, count * across), BF16),
        ],
        input_output_aliases=aliases,
        compiler_params=params(),
        cost_estimate=cost(4 * count * across * channels * depth, 0),
    )(place, *operands)


def far_kernel(n, firsts, place_ref, up_ref, down_ref, gate_ref, mixed_ref, before_ref, *refs):
    outs, local_ref = refs[:-1], refs[-1]
    half, depth = up_ref.shape
    across = 2 * half
    core = place_ref[1]
    start = pl.multiple_of(at_ring(ring_place(place_ref[0], n) + n // 2, n) * across, LANES)
    for base, piece in ((0, up_ref), (half, down_ref)):
        for r in range(0, half, TILE):
            local_ref[base + r : base + r + TILE] = (
                piece[r : r + TILE].astype(F32) * gate_ref[...]
            ).astype(BF16)
    mixed = mixed_ref[:, pl.ds(start, across)]
    for u, first in enumerate(firsts):
        for out_ref, side in ((outs[2 * u], 1 - core), (outs[2 * u + 1], core)):
            width = out_ref.shape[1]
            columns = pl.ds(pl.multiple_of(first + side * width, LANES), width)
            total = jnp.dot(mixed, local_ref[:, columns], preferred_element_type=F32)
            out_ref[...] = (total + before_ref[:, columns]).astype(out_ref.dtype)


def far_parts(n, place, pieces, firsts, widths, gate, mixed, before):
    channels, tokens = mixed.shape
    shapes = []
    for width in widths:
        shapes.append(jax.ShapeDtypeStruct((channels, width), BF16))
        shapes.append(jax.ShapeDtypeStruct((channels, width), F32))
    return pl.pallas_call(
        functools.partial(far_kernel, n, firsts),
        in_specs=[SMEM] + [VMEM] * 5,
        out_specs=[VMEM] * len(shapes),
        out_shape=shapes,
        scratch_shapes=[pltpu.VMEM((tokens // n, before.shape[1]), BF16)],
        compiler_params=params(),
        cost_estimate=cost(1, 1),
    )(place, *pieces, gate, mixed, before)


def far_row_kernel(n, place_ref, up_ref, down_ref, gate_ref, weight_ref, before_ref, grad_ref, local_ref):
    half = up_ref.shape[0]
    across = 2 * half
    start = pl.multiple_of(at_ring(ring_place(place_ref[0], n) + n // 2, n) * across, LANES)
    for base, piece in ((0, up_ref), (half, down_ref)):
        for r in range(0, half, TILE):
            local_ref[base + r : base + r + TILE] = (
                piece[r : r + TILE].astype(F32) * gate_ref[...]
            ).astype(BF16)
    grad_ref[pl.ds(start, across)] = lax.dot_general(
        local_ref[...], weight_ref[...], (((1,), (1,)), ((), ())), preferred_element_type=F32
    )


def far_row(n, place, pieces, gate, weight, before):
    tokens, channels = before.shape
    return pl.pallas_call(
        functools.partial(far_row_kernel, n),
        in_specs=[SMEM] + [VMEM] * 5,
        out_specs=VMEM,
        out_shape=jax.ShapeDtypeStruct(before.shape, F32),
        scratch_shapes=[pltpu.VMEM((tokens // n, weight.shape[1]), BF16)],
        input_output_aliases={5: 0},
        compiler_params=params(),
        cost_estimate=cost(1, 1),
    )(place, *pieces, gate, weight, before)


def grads_kernel(
    scale, grad_ref, gate_ref, value_ref, hidden_ref, taps_ref, out_ref, term_ref, pad_ref
):
    _, height, across, channels = hidden_ref.shape
    clear_edges(pad_ref, height, across)

    @pl.loop(0, channels // LANES)
    def _(c):
        lanes = pl.ds(pl.multiple_of(c * LANES, LANES), LANES)

        @pl.loop(0, height)
        def _(r):
            grad = grad_ref[pl.ds(pl.multiple_of(r * across, across), across), lanes]
            for k, factor in enumerate((gate_ref, value_ref)):
                pad_ref[k, r + 1, PAD : PAD + across] = grad * factor[r, :, lanes].astype(F32)

        weights = taps_ref[:, lanes]
        for k in range(2):

            def row(r, sums):
                sums = list(sums)
                for t in range(across // TILE):
                    w = t * TILE
                    own = hidden_ref[k, r, w : w + TILE, lanes].astype(F32)
                    total = None
                    for i in range(3):
                        for j in range(3):
                            view = pad_ref[k, r + 2 - i, PAD + w + 1 - j : PAD + w + 1 - j + TILE]
                            term = weights[(i * 3 + j) * 2 + k][None, :] * view
                            total = term if total is None else total + term
                            both = view * own
                            sums[i * 3 + j] = sums[i * 3 + j] + (both[:8] + both[8:])
                    out_ref[k, r, w : w + TILE, lanes] = total.astype(BF16)
                return tuple(sums)

            sums = lax.fori_loop(0, height, row, tuple(jnp.zeros((8, LANES), F32) for _ in range(9)))
            for tap in range(9):
                term_ref[tap // 3, tap % 3, k : k + 1, lanes] = scale * jnp.sum(
                    sums[tap], axis=0, keepdims=True
                )


def grads(grad, gate_part, value_part, hidden, taps, scale):
    _, height, across, channels = hidden.shape
    size = height * across * channels
    return pl.pallas_call(
        functools.partial(grads_kernel, scale),
        in_specs=[VMEM] * 5,
        out_specs=[VMEM, VMEM],
        out_shape=[
            jax.ShapeDtypeStruct(hidden.shape, BF16),
            jax.ShapeDtypeStruct((3, 3, 2, channels), F32),
        ],
        scratch_shapes=[pltpu.VMEM((2, height + 2, across + 2 * PAD, LANES), F32)],
        compiler_params=params(),
        cost_estimate=cost(size * 80, size * 20),
    )(grad, gate_part, value_part, hidden, taps)


def put_kernel(firsts, place_ref, *refs):
    count = len(firsts)
    out_ref, sems = refs[-2:]
    copies = []
    for u, first in enumerate(firsts):
        for k, core in ((u, place_ref[1]), (count + u, 1 - place_ref[1])):
            half = refs[k].shape[1]
            columns = pl.ds(pl.multiple_of(first + core * half, LANES), half)
            copies.append(
                pltpu.make_async_copy(refs[k], out_ref.at[:, columns], sems.at[k])
            )
    for copy in copies:
        copy.start()
    for copy in copies:
        copy.wait()


def put(place, mines, others, firsts, whole, shape):
    hbm = pl.BlockSpec(memory_space=pl.ANY)
    arrays = [*mines, *others] + ([] if whole is None else [whole])
    return pl.pallas_call(
        functools.partial(put_kernel, firsts),
        in_specs=[SMEM] + [hbm] * len(arrays),
        out_specs=hbm,
        out_shape=jax.ShapeDtypeStruct(shape, BF16),
        scratch_shapes=[pltpu.SemaphoreType.DMA((2 * len(mines),))],
        input_output_aliases={} if whole is None else {len(arrays): 0},
        compiler_params=params(),
        cost_estimate=cost(1, 1),
    )(place, *arrays)


class Order:
    def __init__(self, token):
        self.token = token

    def after(self, values, waited):
        flat, tree = jax.tree.flatten((values, waited, self.token))
        values, _, self.token = jax.tree.unflatten(tree, lax.optimization_barrier(flat))
        return values


def swap(value, bit):
    n = lax.axis_size("dp")
    return lax.ppermute(value, "dp", [(i, i ^ bit) for i in range(n)])


def sum_far(value, received):
    dp = lax.axis_size("dp")
    value = value.astype(F32) + received.astype(F32)
    bit = 4
    while bit < dp:
        value = value.astype(BF16)
        value = value.astype(F32) + swap(value, bit).astype(F32)
        bit *= 2
    return value


def sum_groups(value):
    dp = lax.axis_size("dp")
    bit = 1
    if dp >= 4:
        one, two, three = swap(value, 1), swap(value, 2), swap(value, 3)
        value = (value + one) + (two + three)
        bit = 4
    while bit < dp:
        value = value + swap(value, bit)
        bit *= 2
    return value


def on_device(hidden_in, conv_weight, proj_weight, out_grad, sample_gate):
    samples, height, across, _, channels = hidden_in.shape
    depth = out_grad.shape[-1]
    n = lax.axis_size("tensor")
    dp = lax.axis_size("dp")
    assert samples == 1 and out_grad.shape[1] == 1 and n % 2 == 0
    assert dp >= 4 and dp & (dp - 1) == 0
    grad_scale = 1.0 / math.sqrt(dp * samples * height * across)
    place = jnp.stack([lax.axis_index("tensor"), lax.rem(lax.axis_index("dp"), 2)]).astype(
        jnp.int32
    )
    own = out_grad.reshape(across, depth)
    hidden = jnp.transpose(hidden_in.reshape(height, across, 2, channels), (2, 0, 1, 3))
    taps = conv_weight.astype(F32).reshape(18, channels)
    order = Order(place)
    ring = ring_order(n)
    right = [(ring[i], ring[(i + 1) % n]) for i in range(n)]
    left = [(ring[i], ring[(i - 1) % n]) for i in range(n)]
    last = n // 2

    def rows(pieces, numbers, before):
        return rows_parts(n, order.token, pieces, numbers, sample_gate, proj_weight, mixed, before)

    half = across // 2
    state = {("up", 0): own[:half], ("down", 1): own[half:], ("up", 1): own[half:], ("down", 0): own[:half]}
    pieces, numbers, before = [own], [0], None
    for stage in range(1, last + 1):
        arrived = {}
        for way, part in state:
            if stage == last and (way, part) not in (("up", 0), ("down", 1)):
                arrived[way, part] = order.after(state[way, part], ())
                continue
            if stage > 1:
                state[way, part] = order.after(state[way, part], ())
            arrived[way, part] = state[way, part]
            state[way, part] = lax.ppermute(state[way, part], "tensor", right if way == "up" else left)
        if stage > 1:
            pieces += [arrived[way, part] for way in ("up", "down") for part in (0, 1)]
            numbers += [1 - stage, stage - 1]
        if stage == 1:
            hidden = order.after(hidden, ())
            gate_part, value_part, mixed = conv_parts(hidden, taps)
            gate_part, value_part, mixed = order.after((gate_part, value_part, mixed), ())
        else:
            before = order.after(rows(pieces, numbers, before), ())
            pieces, numbers = [], []
    far = list(order.after((state["up", 0], state["down", 1]), ()))
    sums, grad = before

    eighth = depth // 8
    widths = [eighth, 3 * eighth // 2, 3 * eighth // 2]
    firsts = [0, 2 * eighth, 5 * eighth]
    pairs, far_sums, mines, others = [], [], [], []

    def begin(u):
        received = order.after(near[u], ())
        pairs.append(order.after((keeps[u] + received.astype(F32)).astype(BF16), ()))
        far_sums.append(swap(pairs[u], 2))

    def finish(u):
        received = order.after(far_sums[u], ())
        mine = (sum_far(pairs[u], received) * grad_scale).astype(BF16)
        mines.append(order.after(mine, ()))
        others.append(swap(mines[u], 1))

    parts = far_parts(n, order.token, far, firsts, widths, sample_gate, mixed, sums)
    parts = order.after(parts, ())
    near = [swap(part, 1) for part in parts[::2]]
    keeps = parts[1::2]
    begin(0)
    begin(1)
    begin(2)
    grad = order.after(grad, ())
    grad = far_row(n, order.token, far, sample_gate, proj_weight, grad)
    hidden_grad, terms = grads(
        grad, gate_part, value_part, hidden, taps, grad_scale
    )
    terms, hidden_grad = order.after((terms, hidden_grad), ())
    total = sum_groups(terms)
    finish(0)
    hidden_grad = with_layout_constraint(
        jnp.transpose(hidden_grad, (1, 2, 0, 3)), Layout(major_to_minor=(0, 1, 2, 3))
    )
    hidden_grad = order.after(hidden_grad, ())
    finish(1)
    total, far_sums[2] = order.after((total, far_sums[2]), ())
    conv_grad = total
    others[0] = order.after(others[0], ())
    others[1] = order.after(others[1], ())
    finish(2)
    shape = (channels, depth)
    whole = put(order.token, mines[:2], others[:2], firsts[:2], None, shape)
    conv_grad = order.after(conv_grad, whole)
    others[2] = order.after(others[2], ())
    whole = put(order.token, mines[2:], others[2:], firsts[2:], whole, shape)
    return (hidden_grad[None], whole, conv_grad)


def solution(mesh):
    in_specs = (
        P("dp", None, None, None, "tensor"),
        P(None, None, None, "tensor"),
        P("tensor", None),
        P("dp", "tensor", None, None),
        P("dp", None),
    )
    out_specs = (
        P("dp", None, None, None, "tensor"),
        P("tensor", None),
        P(None, None, None, "tensor"),
    )
    return jax.shard_map(
        on_device, mesh=mesh, in_specs=in_specs, out_specs=out_specs, check_vma=False
    )
```

```python
import functools
import math

import jax
import jax.numpy as jnp
from jax import lax
from jax.experimental import pallas as pl
from jax.experimental.layout import Layout, with_layout_constraint
from jax.experimental.pallas import tpu as pltpu
from jax.sharding import PartitionSpec as P

F32 = jnp.float32
BF16 = jnp.bfloat16
PAD = 8
TILE = 16
LANES = 128
VMEM_BYTES = 20 * 1024 * 1024
VMEM = pl.BlockSpec(memory_space=pltpu.VMEM)
SMEM = pl.BlockSpec(memory_space=pltpu.SMEM)


def ring_order(n):
    return [2 * i if i < n // 2 else 2 * (n - 1 - i) + 1 for i in range(n)]


def at_ring(position, n):
    position = lax.rem(position + 2 * n, n)
    return jnp.where(position < n // 2, 2 * position, 2 * (n - 1 - position) + 1)


def ring_place(index, n):
    half = index // 2
    return jnp.where(lax.rem(index, 2) == 0, half, n - 1 - half)


def params(limit=VMEM_BYTES):
    return pltpu.CompilerParams(vmem_limit_bytes=limit)


def cost(flops, moved, transcendentals=0):
    return pl.CostEstimate(flops=1, bytes_accessed=1, transcendentals=0)


def clear_edges(pad_ref, height, across):
    lanes = pad_ref.shape[-1]
    for k in range(2):
        pad_ref[k, 0] = jnp.zeros(pad_ref.shape[2:], F32)
        pad_ref[k, height + 1] = jnp.zeros(pad_ref.shape[2:], F32)

        @pl.loop(0, height)
        def _(r):
            pad_ref[k, r + 1, 0:PAD] = jnp.zeros((PAD, lanes), F32)
            pad_ref[k, r + 1, PAD + across : 2 * PAD + across] = jnp.zeros((PAD, lanes), F32)


def conv_kernel(first, count, hidden_ref, weight_ref, *refs):
    gate_ref, value_ref, mixed_ref, pad_ref = refs[-4:]
    _, height, across, channels = hidden_ref.shape
    clear_edges(pad_ref, height, across)

    @pl.loop(first, first + count)
    def _(c):
        lanes = pl.ds(pl.multiple_of(c * LANES, LANES), LANES)

        @pl.loop(0, height)
        def _(r):
            for k in range(2):
                pad_ref[k, r + 1, PAD : PAD + across] = hidden_ref[k, r, :, lanes].astype(F32)

        weights = weight_ref[:, lanes]

        @pl.loop(0, height)
        def _(r):
            mixed = []
            for t in range(across // TILE):
                w = t * TILE
                parts = []
                for k in range(2):
                    total = None
                    for i in range(3):
                        for j in range(3):
                            view = pad_ref[k, r + i, PAD + w + j - 1 : PAD + w + j - 1 + TILE]
                            term = weights[(i * 3 + j) * 2 + k][None, :] * view
                            total = term if total is None else total + term
                    parts.append(total)
                value, gate = parts
                sig = 1.0 / (1.0 + jnp.exp(-gate))
                gated = gate * sig
                gate_ref[r, w : w + TILE, lanes] = gated.astype(BF16)
                value_ref[r, w : w + TILE, lanes] = (
                    value * sig * (1.0 + gate * (1.0 - sig))
                ).astype(BF16)
                mixed.append((value * gated).astype(BF16))
            tokens = pl.ds(pl.multiple_of(r * across, LANES), across)
            mixed_ref[lanes, tokens] = jnp.concatenate(mixed, axis=0).T


def conv_parts(hidden, weights, first, count, before=()):
    _, height, across, channels = hidden.shape
    return pl.pallas_call(
        functools.partial(conv_kernel, first, count),
        in_specs=[VMEM] * (2 + len(before)),
        out_specs=[VMEM] * 3,
        out_shape=[
            jax.ShapeDtypeStruct((height, across, channels), BF16),
            jax.ShapeDtypeStruct((height, across, channels), BF16),
            jax.ShapeDtypeStruct((channels, height * across), BF16),
        ],
        scratch_shapes=[pltpu.VMEM((2, height + 2, across + 2 * PAD, LANES), F32)],
        input_output_aliases={2 + k: k for k in range(len(before))},
        compiler_params=params(),
        cost_estimate=cost(1, 1),
    )(hidden, weights, *before)


def rows_kernel(n, parts, numbers, added, place_ref, *refs):
    count = len(numbers)
    pieces, refs = refs[:parts], refs[parts:]
    gate_ref, weight_ref, mixed_ref = refs[:3]
    sums_ref, grad_ref, local_ref, side_ref = refs[-4:]
    before_ref = refs[3] if added else None
    across = local_ref.shape[0] // count
    depth = local_ref.shape[1]
    spot = ring_place(place_ref[0], n)
    starts = [
        pl.multiple_of(at_ring(spot + step, n) * across, LANES) for step in numbers
    ]
    base = 0
    for piece in pieces:
        for r in range(0, piece.shape[0], TILE):
            local_ref[base + r : base + r + TILE] = (
                piece[r : r + TILE].astype(F32) * gate_ref[...]
            ).astype(BF16)
        base += piece.shape[0]
    for k, start in enumerate(starts):
        side_ref[:, k * across : (k + 1) * across] = mixed_ref[:, pl.ds(start, across)]
    block = min(depth, 512)
    for c in range(0, depth, block):
        total = jnp.dot(
            side_ref[...], local_ref[:, c : c + block], preferred_element_type=F32
        )
        if added:
            total = total + before_ref[:, c : c + block]
        sums_ref[:, c : c + block] = total
    product = lax.dot_general(
        local_ref[...], weight_ref[...], (((1,), (1,)), ((), ())), preferred_element_type=F32
    )
    for k, start in enumerate(starts):
        grad_ref[pl.ds(start, across)] = product[k * across : (k + 1) * across]


def rows_parts(n, place, pieces, numbers, gate, weight, mixed, before=None):
    depth = pieces[0].shape[1]
    channels, tokens = mixed.shape
    count, across = len(numbers), tokens // n
    operands = [*pieces, gate, weight, mixed]
    aliases = {}
    if before is not None:
        aliases = {len(operands) + 1: 0, len(operands) + 2: 1}
        operands += before
    return pl.pallas_call(
        functools.partial(rows_kernel, n, len(pieces), numbers, before is not None),
        in_specs=[SMEM] + [VMEM] * len(operands),
        out_specs=[VMEM] * 2,
        out_shape=[
            jax.ShapeDtypeStruct((channels, depth), F32),
            jax.ShapeDtypeStruct((tokens, channels), F32),
        ],
        scratch_shapes=[
            pltpu.VMEM((count * across, depth), BF16),
            pltpu.VMEM((channels, count * across), BF16),
        ],
        input_output_aliases=aliases,
        compiler_params=params(),
        cost_estimate=cost(4 * count * across * channels * depth, 0),
    )(place, *operands)


def far_kernel(n, firsts, place_ref, up_ref, down_ref, gate_ref, mixed_ref, before_ref, *refs):
    outs, local_ref = refs[:-1], refs[-1]
    half, depth = up_ref.shape
    across = 2 * half
    core = place_ref[1]
    start = pl.multiple_of(at_ring(ring_place(place_ref[0], n) + n // 2, n) * across, LANES)
    for base, piece in ((0, up_ref), (half, down_ref)):
        for r in range(0, half, TILE):
            local_ref[base + r : base + r + TILE] = (
                piece[r : r + TILE].astype(F32) * gate_ref[...]
            ).astype(BF16)
    mixed = mixed_ref[:, pl.ds(start, across)]
    for u, first in enumerate(firsts):
        for out_ref, side in ((outs[2 * u], 1 - core), (outs[2 * u + 1], core)):
            width = out_ref.shape[1]
            columns = pl.ds(pl.multiple_of(first + side * width, LANES), width)
            total = jnp.dot(mixed, local_ref[:, columns], preferred_element_type=F32)
            out_ref[...] = (total + before_ref[:, columns]).astype(out_ref.dtype)


def far_parts(n, place, pieces, firsts, widths, gate, mixed, before):
    channels, tokens = mixed.shape
    shapes = []
    for width in widths:
        shapes.append(jax.ShapeDtypeStruct((channels, width), BF16))
        shapes.append(jax.ShapeDtypeStruct((channels, width), F32))
    return pl.pallas_call(
        functools.partial(far_kernel, n, firsts),
        in_specs=[SMEM] + [VMEM] * 5,
        out_specs=[VMEM] * len(shapes),
        out_shape=shapes,
        scratch_shapes=[pltpu.VMEM((tokens // n, before.shape[1]), BF16)],
        compiler_params=params(),
        cost_estimate=cost(1, 1),
    )(place, *pieces, gate, mixed, before)


def far_row_kernel(n, place_ref, up_ref, down_ref, gate_ref, weight_ref, before_ref, grad_ref, local_ref):
    half = up_ref.shape[0]
    across = 2 * half
    start = pl.multiple_of(at_ring(ring_place(place_ref[0], n) + n // 2, n) * across, LANES)
    for base, piece in ((0, up_ref), (half, down_ref)):
        for r in range(0, half, TILE):
            local_ref[base + r : base + r + TILE] = (
                piece[r : r + TILE].astype(F32) * gate_ref[...]
            ).astype(BF16)
    grad_ref[pl.ds(start, across)] = lax.dot_general(
        local_ref[...], weight_ref[...], (((1,), (1,)), ((), ())), preferred_element_type=F32
    )


def far_row(n, place, pieces, gate, weight, before):
    tokens, channels = before.shape
    return pl.pallas_call(
        functools.partial(far_row_kernel, n),
        in_specs=[SMEM] + [VMEM] * 5,
        out_specs=VMEM,
        out_shape=jax.ShapeDtypeStruct(before.shape, F32),
        scratch_shapes=[pltpu.VMEM((tokens // n, weight.shape[1]), BF16)],
        input_output_aliases={5: 0},
        compiler_params=params(),
        cost_estimate=cost(1, 1),
    )(place, *pieces, gate, weight, before)


def grads_kernel(
    scale, grad_ref, gate_ref, value_ref, hidden_ref, taps_ref, out_ref, term_ref, pad_ref
):
    _, height, across, channels = hidden_ref.shape
    clear_edges(pad_ref, height, across)

    @pl.loop(0, channels // LANES)
    def _(c):
        lanes = pl.ds(pl.multiple_of(c * LANES, LANES), LANES)

        @pl.loop(0, height)
        def _(r):
            grad = grad_ref[pl.ds(pl.multiple_of(r * across, across), across), lanes]
            for k, factor in enumerate((gate_ref, value_ref)):
                pad_ref[k, r + 1, PAD : PAD + across] = grad * factor[r, :, lanes].astype(F32)

        weights = taps_ref[:, lanes]
        for k in range(2):

            def row(r, sums):
                sums = list(sums)
                for t in range(across // TILE):
                    w = t * TILE
                    own = hidden_ref[k, r, w : w + TILE, lanes].astype(F32)
                    total = None
                    for i in range(3):
                        for j in range(3):
                            view = pad_ref[k, r + 2 - i, PAD + w + 1 - j : PAD + w + 1 - j + TILE]
                            term = weights[(i * 3 + j) * 2 + k][None, :] * view
                            total = term if total is None else total + term
                            both = view * own
                            sums[i * 3 + j] = sums[i * 3 + j] + (both[:8] + both[8:])
                    out_ref[k, r, w : w + TILE, lanes] = total.astype(BF16)
                return tuple(sums)

            sums = lax.fori_loop(0, height, row, tuple(jnp.zeros((8, LANES), F32) for _ in range(9)))
            for tap in range(9):
                term_ref[tap // 3, tap % 3, k : k + 1, lanes] = scale * jnp.sum(
                    sums[tap], axis=0, keepdims=True
                )


def grads(grad, gate_part, value_part, hidden, taps, scale):
    _, height, across, channels = hidden.shape
    size = height * across * channels
    return pl.pallas_call(
        functools.partial(grads_kernel, scale),
        in_specs=[VMEM] * 5,
        out_specs=[VMEM, VMEM],
        out_shape=[
            jax.ShapeDtypeStruct(hidden.shape, BF16),
            jax.ShapeDtypeStruct((3, 3, 2, channels), F32),
        ],
        scratch_shapes=[pltpu.VMEM((2, height + 2, across + 2 * PAD, LANES), F32)],
        compiler_params=params(),
        cost_estimate=cost(size * 80, size * 20),
    )(grad, gate_part, value_part, hidden, taps)


def put_kernel(firsts, given, place_ref, *refs):
    count = len(firsts)
    out_ref, sems = refs[-2:]
    copies = []
    for k in range(count + given):
        half = refs[k].shape[1]
        core = place_ref[1] if k < count else 1 - place_ref[1]
        columns = pl.ds(pl.multiple_of(firsts[k % count] + core * half, LANES), half)
        copies.append(pltpu.make_async_copy(refs[k], out_ref.at[:, columns], sems.at[k]))
    for copy in copies:
        copy.start()
    for copy in copies:
        copy.wait()


def put(place, mines, others, firsts, shape):
    hbm = pl.BlockSpec(memory_space=pl.ANY)
    arrays = [*mines, *others]
    return pl.pallas_call(
        functools.partial(put_kernel, firsts, len(others)),
        in_specs=[SMEM] + [hbm] * len(arrays),
        out_specs=hbm,
        out_shape=jax.ShapeDtypeStruct(shape, BF16),
        scratch_shapes=[pltpu.SemaphoreType.DMA((len(arrays),))],
        compiler_params=params(),
        cost_estimate=cost(1, 1),
    )(place, *arrays)


class Order:
    def __init__(self, token):
        self.token = token

    def after(self, values, waited):
        flat, tree = jax.tree.flatten((values, waited, self.token))
        values, _, self.token = jax.tree.unflatten(tree, lax.optimization_barrier(flat))
        return values


def swap(value, bit):
    n = lax.axis_size("dp")
    return lax.ppermute(value, "dp", [(i, i ^ bit) for i in range(n)])


def sum_far(value, received):
    dp = lax.axis_size("dp")
    value = value.astype(F32) + received.astype(F32)
    bit = 4
    while bit < dp:
        value = value.astype(BF16)
        value = value.astype(F32) + swap(value, bit).astype(F32)
        bit *= 2
    return value


def on_device(hidden_in, conv_weight, proj_weight, out_grad, sample_gate):
    samples, height, across, _, channels = hidden_in.shape
    depth = out_grad.shape[-1]
    n = lax.axis_size("tensor")
    dp = lax.axis_size("dp")
    assert samples == 1 and out_grad.shape[1] == 1 and n % 2 == 0
    assert dp >= 4 and dp & (dp - 1) == 0
    grad_scale = 1.0 / math.sqrt(dp * samples * height * across)
    place = jnp.stack([lax.axis_index("tensor"), lax.rem(lax.axis_index("dp"), 2)]).astype(
        jnp.int32
    )
    own = out_grad.reshape(across, depth)
    hidden = jnp.transpose(hidden_in.reshape(height, across, 2, channels), (2, 0, 1, 3))
    taps = conv_weight.astype(F32).reshape(18, channels)
    order = Order(place)
    ring = ring_order(n)
    right = [(ring[i], ring[(i + 1) % n]) for i in range(n)]
    left = [(ring[i], ring[(i - 1) % n]) for i in range(n)]
    last = n // 2

    def rows(pieces, numbers, before):
        return rows_parts(n, order.token, pieces, numbers, sample_gate, proj_weight, mixed, before)

    half = across // 2
    state = {("up", 0): own[:half], ("down", 1): own[half:], ("up", 1): own[half:], ("down", 0): own[:half]}
    pieces, numbers, before = [own], [0], None
    blocks = channels // LANES
    early = blocks - blocks // 4
    for stage in range(1, last + 1):
        arrived = {}
        for way, part in state:
            if stage == last and (way, part) not in (("up", 0), ("down", 1)):
                arrived[way, part] = order.after(state[way, part], ())
                continue
            if stage > 1:
                state[way, part] = order.after(state[way, part], ())
            arrived[way, part] = state[way, part]
            state[way, part] = lax.ppermute(state[way, part], "tensor", right if way == "up" else left)
        if stage > 1:
            pieces += [arrived[way, part] for way in ("up", "down") for part in (0, 1)]
            numbers += [1 - stage, stage - 1]
        if stage == 1:
            hidden = order.after(hidden, ())
            conv = order.after(conv_parts(hidden, taps, 0, early), ())
        else:
            if stage == 2 and early < blocks:
                conv = order.after(conv_parts(hidden, taps, early, blocks - early, conv), ())
            gate_part, value_part, mixed = conv
            before = order.after(rows(pieces, numbers, before), ())
            pieces, numbers = [], []
    far = list(order.after((state["up", 0], state["down", 1]), ()))
    sums, grad = before

    eighth = depth // 8
    widths = [eighth, 3 * eighth // 2, 3 * eighth // 2]
    firsts = [0, 2 * eighth, 5 * eighth]
    pairs, far_sums, mines, others = [], [], [], []

    def begin(u):
        received = order.after(near[u], ())
        pairs.append(order.after((keeps[u] + received.astype(F32)).astype(BF16), ()))
        far_sums.append(swap(pairs[u], 2))

    def finish(u):
        received = order.after(far_sums[u], ())
        mine = (sum_far(pairs[u], received) * grad_scale).astype(BF16)
        mines.append(order.after(mine, ()))
        others.append(swap(mines[u], 1))

    parts = far_parts(n, order.token, far, firsts, widths, sample_gate, mixed, sums)
    parts = order.after(parts, ())
    near = [swap(part, 1) for part in parts[::2]]
    keeps = parts[1::2]
    begin(0)
    begin(1)
    begin(2)
    grad = order.after(grad, ())
    grad = far_row(n, order.token, far, sample_gate, proj_weight, grad)
    hidden_grad, terms = grads(
        grad, gate_part, value_part, hidden, taps, grad_scale
    )
    terms, hidden_grad = order.after((terms, hidden_grad), ())
    received = swap(terms, 1)
    finish(0)
    hidden_grad = with_layout_constraint(
        jnp.transpose(hidden_grad, (1, 2, 0, 3)), Layout(major_to_minor=(0, 1, 2, 3))
    )
    hidden_grad = order.after(hidden_grad, ())
    finish(1)
    received = order.after(received, ())
    terms = order.after(terms + received, ())
    received = swap(terms, 2)
    received, far_sums[2] = order.after((received, far_sums[2]), ())
    conv_grad = terms + received
    bit = 4
    while bit < dp:
        conv_grad = conv_grad + swap(conv_grad, bit)
        bit *= 2
    others[0] = order.after(others[0], ())
    others[1] = order.after(others[1], ())
    finish(2)
    shape = (channels, depth)
    whole = put(order.token, mines, others[:2], firsts, shape)
    whole, others[2] = order.after((whole, others[2]), ())
    column = firsts[2] + (1 - place[1]) * widths[2]
    whole = lax.dynamic_update_slice(whole, others[2], (0, column))
    return (hidden_grad[None], whole, conv_grad)


def solution(mesh):
    in_specs = (
        P("dp", None, None, None, "tensor"),
        P(None, None, None, "tensor"),
        P("tensor", None),
        P("dp", "tensor", None, None),
        P("dp", None),
    )
    out_specs = (
        P("dp", None, None, None, "tensor"),
        P("tensor", None),
        P(None, None, None, "tensor"),
    )
    return jax.shard_map(
        on_device, mesh=mesh, in_specs=in_specs, out_specs=out_specs, check_vma=False
    )
```

```python
import functools
import math

import jax
import jax.numpy as jnp
from jax import lax
from jax.experimental import pallas as pl
from jax.experimental.layout import Layout, with_layout_constraint
from jax.experimental.pallas import tpu as pltpu
from jax.sharding import PartitionSpec as P

F32 = jnp.float32
BF16 = jnp.bfloat16
PAD = 8
TILE = 16
LANES = 128
VMEM_BYTES = 20 * 1024 * 1024
VMEM = pl.BlockSpec(memory_space=pltpu.VMEM)
SMEM = pl.BlockSpec(memory_space=pltpu.SMEM)


def ring_order(n):
    return [2 * i if i < n // 2 else 2 * (n - 1 - i) + 1 for i in range(n)]


def at_ring(position, n):
    position = lax.rem(position + 2 * n, n)
    return jnp.where(position < n // 2, 2 * position, 2 * (n - 1 - position) + 1)


def ring_place(index, n):
    half = index // 2
    return jnp.where(lax.rem(index, 2) == 0, half, n - 1 - half)


def params(limit=VMEM_BYTES):
    return pltpu.CompilerParams(vmem_limit_bytes=limit)


def cost(flops, moved, transcendentals=0):
    return pl.CostEstimate(flops=1, bytes_accessed=1, transcendentals=0)


def clear_edges(pad_ref, height, across):
    lanes = pad_ref.shape[-1]
    for k in range(2):
        pad_ref[k, 0] = jnp.zeros(pad_ref.shape[2:], F32)
        pad_ref[k, height + 1] = jnp.zeros(pad_ref.shape[2:], F32)

        @pl.loop(0, height)
        def _(r):
            pad_ref[k, r + 1, 0:PAD] = jnp.zeros((PAD, lanes), F32)
            pad_ref[k, r + 1, PAD + across : 2 * PAD + across] = jnp.zeros((PAD, lanes), F32)


def conv_kernel(first, count, hidden_ref, weight_ref, *refs):
    gate_ref, value_ref, mixed_ref, pad_ref = refs[-4:]
    _, height, across, channels = hidden_ref.shape
    clear_edges(pad_ref, height, across)

    @pl.loop(first, first + count)
    def _(c):
        lanes = pl.ds(pl.multiple_of(c * LANES, LANES), LANES)

        @pl.loop(0, height)
        def _(r):
            for k in range(2):
                pad_ref[k, r + 1, PAD : PAD + across] = hidden_ref[k, r, :, lanes].astype(F32)

        weights = weight_ref[:, lanes]

        @pl.loop(0, height)
        def _(r):
            mixed = []
            for t in range(across // TILE):
                w = t * TILE
                parts = []
                for k in range(2):
                    total = None
                    for i in range(3):
                        for j in range(3):
                            view = pad_ref[k, r + i, PAD + w + j - 1 : PAD + w + j - 1 + TILE]
                            term = weights[(i * 3 + j) * 2 + k][None, :] * view
                            total = term if total is None else total + term
                    parts.append(total)
                value, gate = parts
                sig = 1.0 / (1.0 + jnp.exp(-gate))
                gated = gate * sig
                gate_ref[r, w : w + TILE, lanes] = gated.astype(BF16)
                value_ref[r, w : w + TILE, lanes] = (
                    value * sig * (1.0 + gate * (1.0 - sig))
                ).astype(BF16)
                mixed.append((value * gated).astype(BF16))
            tokens = pl.ds(pl.multiple_of(r * across, LANES), across)
            mixed_ref[lanes, tokens] = jnp.concatenate(mixed, axis=0).T


def conv_parts(hidden, weights, first, count, before=()):
    _, height, across, channels = hidden.shape
    return pl.pallas_call(
        functools.partial(conv_kernel, first, count),
        in_specs=[VMEM] * (2 + len(before)),
        out_specs=[VMEM] * 3,
        out_shape=[
            jax.ShapeDtypeStruct((height, across, channels), BF16),
            jax.ShapeDtypeStruct((height, across, channels), BF16),
            jax.ShapeDtypeStruct((channels, height * across), BF16),
        ],
        scratch_shapes=[pltpu.VMEM((2, height + 2, across + 2 * PAD, LANES), F32)],
        input_output_aliases={2 + k: k for k in range(len(before))},
        compiler_params=params(),
        cost_estimate=cost(1, 1),
    )(hidden, weights, *before)


def rows_kernel(n, parts, numbers, added, place_ref, *refs):
    count = len(numbers)
    pieces, refs = refs[:parts], refs[parts:]
    gate_ref, weight_ref, mixed_ref = refs[:3]
    sums_ref, grad_ref, local_ref, side_ref = refs[-4:]
    before_ref = refs[3] if added else None
    across = local_ref.shape[0] // count
    depth = local_ref.shape[1]
    spot = ring_place(place_ref[0], n)
    starts = [
        pl.multiple_of(at_ring(spot + step, n) * across, LANES) for step in numbers
    ]
    base = 0
    for piece in pieces:
        for r in range(0, piece.shape[0], TILE):
            local_ref[base + r : base + r + TILE] = (
                piece[r : r + TILE].astype(F32) * gate_ref[...]
            ).astype(BF16)
        base += piece.shape[0]
    for k, start in enumerate(starts):
        side_ref[:, k * across : (k + 1) * across] = mixed_ref[:, pl.ds(start, across)]
    block = min(depth, 512)
    for c in range(0, depth, block):
        total = jnp.dot(
            side_ref[...], local_ref[:, c : c + block], preferred_element_type=F32
        )
        if added:
            total = total + before_ref[:, c : c + block]
        sums_ref[:, c : c + block] = total
    product = lax.dot_general(
        local_ref[...], weight_ref[...], (((1,), (1,)), ((), ())), preferred_element_type=F32
    )
    for k, start in enumerate(starts):
        grad_ref[pl.ds(start, across)] = product[k * across : (k + 1) * across]


def rows_parts(n, place, pieces, numbers, gate, weight, mixed, before=None):
    depth = pieces[0].shape[1]
    channels, tokens = mixed.shape
    count, across = len(numbers), tokens // n
    operands = [*pieces, gate, weight, mixed]
    aliases = {}
    if before is not None:
        aliases = {len(operands) + 1: 0, len(operands) + 2: 1}
        operands += before
    return pl.pallas_call(
        functools.partial(rows_kernel, n, len(pieces), numbers, before is not None),
        in_specs=[SMEM] + [VMEM] * len(operands),
        out_specs=[VMEM] * 2,
        out_shape=[
            jax.ShapeDtypeStruct((channels, depth), F32),
            jax.ShapeDtypeStruct((tokens, channels), F32),
        ],
        scratch_shapes=[
            pltpu.VMEM((count * across, depth), BF16),
            pltpu.VMEM((channels, count * across), BF16),
        ],
        input_output_aliases=aliases,
        compiler_params=params(),
        cost_estimate=cost(4 * count * across * channels * depth, 0),
    )(place, *operands)


def far_kernel(n, firsts, place_ref, up_ref, down_ref, gate_ref, mixed_ref, before_ref, *refs):
    outs, local_ref = refs[:-1], refs[-1]
    half, depth = up_ref.shape
    across = 2 * half
    core = place_ref[1]
    start = pl.multiple_of(at_ring(ring_place(place_ref[0], n) + n // 2, n) * across, LANES)
    for base, piece in ((0, up_ref), (half, down_ref)):
        for r in range(0, half, TILE):
            local_ref[base + r : base + r + TILE] = (
                piece[r : r + TILE].astype(F32) * gate_ref[...]
            ).astype(BF16)
    mixed = mixed_ref[:, pl.ds(start, across)]
    for u, first in enumerate(firsts):
        for out_ref, side in ((outs[2 * u], 1 - core), (outs[2 * u + 1], core)):
            width = out_ref.shape[1]
            columns = pl.ds(pl.multiple_of(first + side * width, LANES), width)
            total = jnp.dot(mixed, local_ref[:, columns], preferred_element_type=F32)
            out_ref[...] = (total + before_ref[:, columns]).astype(out_ref.dtype)


def far_parts(n, place, pieces, firsts, widths, gate, mixed, before):
    channels, tokens = mixed.shape
    shapes = []
    for width in widths:
        shapes.append(jax.ShapeDtypeStruct((channels, width), BF16))
        shapes.append(jax.ShapeDtypeStruct((channels, width), F32))
    return pl.pallas_call(
        functools.partial(far_kernel, n, firsts),
        in_specs=[SMEM] + [VMEM] * 5,
        out_specs=[VMEM] * len(shapes),
        out_shape=shapes,
        scratch_shapes=[pltpu.VMEM((tokens // n, before.shape[1]), BF16)],
        compiler_params=params(),
        cost_estimate=cost(1, 1),
    )(place, *pieces, gate, mixed, before)


def far_row_kernel(n, place_ref, up_ref, down_ref, gate_ref, weight_ref, before_ref, grad_ref, local_ref):
    half = up_ref.shape[0]
    across = 2 * half
    start = pl.multiple_of(at_ring(ring_place(place_ref[0], n) + n // 2, n) * across, LANES)
    for base, piece in ((0, up_ref), (half, down_ref)):
        for r in range(0, half, TILE):
            local_ref[base + r : base + r + TILE] = (
                piece[r : r + TILE].astype(F32) * gate_ref[...]
            ).astype(BF16)
    grad_ref[pl.ds(start, across)] = lax.dot_general(
        local_ref[...], weight_ref[...], (((1,), (1,)), ((), ())), preferred_element_type=F32
    )


def far_row(n, place, pieces, gate, weight, before):
    tokens, channels = before.shape
    return pl.pallas_call(
        functools.partial(far_row_kernel, n),
        in_specs=[SMEM] + [VMEM] * 5,
        out_specs=VMEM,
        out_shape=jax.ShapeDtypeStruct(before.shape, F32),
        scratch_shapes=[pltpu.VMEM((tokens // n, weight.shape[1]), BF16)],
        input_output_aliases={5: 0},
        compiler_params=params(),
        cost_estimate=cost(1, 1),
    )(place, *pieces, gate, weight, before)


def grads_kernel(
    scale, grad_ref, gate_ref, value_ref, hidden_ref, taps_ref, out_ref, term_ref, pad_ref
):
    _, height, across, channels = hidden_ref.shape
    clear_edges(pad_ref, height, across)

    @pl.loop(0, channels // LANES)
    def _(c):
        lanes = pl.ds(pl.multiple_of(c * LANES, LANES), LANES)

        @pl.loop(0, height)
        def _(r):
            grad = grad_ref[pl.ds(pl.multiple_of(r * across, across), across), lanes]
            for k, factor in enumerate((gate_ref, value_ref)):
                pad_ref[k, r + 1, PAD : PAD + across] = grad * factor[r, :, lanes].astype(F32)

        weights = taps_ref[:, lanes]
        for k in range(2):

            def row(r, sums):
                sums = list(sums)
                for t in range(across // TILE):
                    w = t * TILE
                    own = hidden_ref[k, r, w : w + TILE, lanes].astype(F32)
                    total = None
                    for i in range(3):
                        for j in range(3):
                            view = pad_ref[k, r + 2 - i, PAD + w + 1 - j : PAD + w + 1 - j + TILE]
                            term = weights[(i * 3 + j) * 2 + k][None, :] * view
                            total = term if total is None else total + term
                            both = view * own
                            sums[i * 3 + j] = sums[i * 3 + j] + (both[:8] + both[8:])
                    out_ref[k, r, w : w + TILE, lanes] = total.astype(BF16)
                return tuple(sums)

            sums = lax.fori_loop(0, height, row, tuple(jnp.zeros((8, LANES), F32) for _ in range(9)))
            for tap in range(9):
                term_ref[tap // 3, tap % 3, k : k + 1, lanes] = scale * jnp.sum(
                    sums[tap], axis=0, keepdims=True
                )


def grads(grad, gate_part, value_part, hidden, taps, scale):
    _, height, across, channels = hidden.shape
    size = height * across * channels
    return pl.pallas_call(
        functools.partial(grads_kernel, scale),
        in_specs=[VMEM] * 5,
        out_specs=[VMEM, VMEM],
        out_shape=[
            jax.ShapeDtypeStruct(hidden.shape, BF16),
            jax.ShapeDtypeStruct((3, 3, 2, channels), F32),
        ],
        scratch_shapes=[pltpu.VMEM((2, height + 2, across + 2 * PAD, LANES), F32)],
        compiler_params=params(),
        cost_estimate=cost(size * 80, size * 20),
    )(grad, gate_part, value_part, hidden, taps)


def put_kernel(firsts, given, place_ref, *refs):
    count = len(firsts)
    one_ref, two_ref, out_ref, total_ref, shares_ref, sems, share_sems = refs[-7:]
    shares = [
        pltpu.make_async_copy(ref, shares_ref.at[k], share_sems.at[k])
        for k, ref in enumerate((one_ref, two_ref))
    ]
    for copy in shares:
        copy.start()
    copies = []
    for k in range(count + given):
        half = refs[k].shape[1]
        core = place_ref[1] if k < count else 1 - place_ref[1]
        columns = pl.ds(pl.multiple_of(firsts[k % count] + core * half, LANES), half)
        copies.append(pltpu.make_async_copy(refs[k], out_ref.at[:, columns], sems.at[k]))
    for copy in copies:
        copy.start()
    for copy in shares:
        copy.wait()
    shares_ref[2] = shares_ref[0] + shares_ref[1]
    total = pltpu.make_async_copy(shares_ref.at[2], total_ref, share_sems.at[2])
    total.start()
    for copy in copies:
        copy.wait()
    total.wait()


def put(place, mines, others, firsts, shape, one, two):
    hbm = pl.BlockSpec(memory_space=pl.ANY)
    arrays = [*mines, *others]
    return pl.pallas_call(
        functools.partial(put_kernel, firsts, len(others)),
        in_specs=[SMEM] + [hbm] * (len(arrays) + 2),
        out_specs=[hbm, hbm],
        out_shape=[jax.ShapeDtypeStruct(shape, BF16), jax.ShapeDtypeStruct(one.shape, F32)],
        scratch_shapes=[
            pltpu.VMEM((3, *one.shape), F32),
            pltpu.SemaphoreType.DMA((len(arrays),)),
            pltpu.SemaphoreType.DMA((3,)),
        ],
        compiler_params=params(),
        cost_estimate=cost(1, 1),
    )(place, *arrays, one, two)


class Order:
    def __init__(self, token):
        self.token = token

    def after(self, values, waited):
        flat, tree = jax.tree.flatten((values, waited, self.token))
        values, _, self.token = jax.tree.unflatten(tree, lax.optimization_barrier(flat))
        return values


def swap(value, bit):
    n = lax.axis_size("dp")
    return lax.ppermute(value, "dp", [(i, i ^ bit) for i in range(n)])


def sum_far(value, received):
    dp = lax.axis_size("dp")
    value = value.astype(F32) + received.astype(F32)
    bit = 4
    while bit < dp:
        value = value.astype(BF16)
        value = value.astype(F32) + swap(value, bit).astype(F32)
        bit *= 2
    return value


def on_device(hidden_in, conv_weight, proj_weight, out_grad, sample_gate):
    samples, height, across, _, channels = hidden_in.shape
    depth = out_grad.shape[-1]
    n = lax.axis_size("tensor")
    dp = lax.axis_size("dp")
    assert samples == 1 and out_grad.shape[1] == 1 and n % 2 == 0
    assert dp >= 4 and dp & (dp - 1) == 0
    grad_scale = 1.0 / math.sqrt(dp * samples * height * across)
    place = jnp.stack([lax.axis_index("tensor"), lax.rem(lax.axis_index("dp"), 2)]).astype(
        jnp.int32
    )
    own = out_grad.reshape(across, depth)
    hidden = jnp.transpose(hidden_in.reshape(height, across, 2, channels), (2, 0, 1, 3))
    taps = conv_weight.astype(F32).reshape(18, channels)
    order = Order(place)
    ring = ring_order(n)
    right = [(ring[i], ring[(i + 1) % n]) for i in range(n)]
    left = [(ring[i], ring[(i - 1) % n]) for i in range(n)]
    last = n // 2

    def rows(pieces, numbers, before):
        return rows_parts(n, order.token, pieces, numbers, sample_gate, proj_weight, mixed, before)

    half = across // 2
    state = {("up", 0): own[:half], ("down", 1): own[half:], ("up", 1): own[half:], ("down", 0): own[:half]}
    pieces, numbers, before = [own], [0], None
    blocks = channels // LANES
    early = blocks - blocks // 4
    for stage in range(1, last + 1):
        arrived = {}
        for way, part in state:
            if stage == last and (way, part) not in (("up", 0), ("down", 1)):
                arrived[way, part] = order.after(state[way, part], ())
                continue
            if stage > 1:
                state[way, part] = order.after(state[way, part], ())
            arrived[way, part] = state[way, part]
            state[way, part] = lax.ppermute(state[way, part], "tensor", right if way == "up" else left)
        if stage > 1:
            pieces += [arrived[way, part] for way in ("up", "down") for part in (0, 1)]
            numbers += [1 - stage, stage - 1]
        if stage == 1:
            hidden = order.after(hidden, ())
            conv = order.after(conv_parts(hidden, taps, 0, early), ())
        else:
            if stage == 2 and early < blocks:
                conv = order.after(conv_parts(hidden, taps, early, blocks - early, conv), ())
            gate_part, value_part, mixed = conv
            before = order.after(rows(pieces, numbers, before), ())
            pieces, numbers = [], []
    far = list(order.after((state["up", 0], state["down", 1]), ()))
    sums, grad = before

    eighth = depth // 8
    widths = [2 * eighth // 2, 3 * eighth // 2, 3 * eighth // 2]
    firsts = [sum(widths[:u]) * 2 for u in range(len(widths))]
    pairs, far_sums, mines, others = [], [], [], []

    def begin(u):
        received = order.after(near[u], ())
        pairs.append(order.after((keeps[u] + received.astype(F32)).astype(BF16), ()))
        far_sums.append(swap(pairs[u], 2))

    def finish(u):
        received = order.after(far_sums[u], ())
        mine = (sum_far(pairs[u], received) * grad_scale).astype(BF16)
        mines.append(order.after(mine, ()))
        others.append(swap(mines[u], 1))

    parts = far_parts(n, order.token, far, firsts, widths, sample_gate, mixed, sums)
    parts = order.after(parts, ())
    near = [swap(part, 1) for part in parts[::2]]
    keeps = parts[1::2]
    begin(0)
    begin(1)
    begin(2)
    grad = order.after(grad, ())
    grad = far_row(n, order.token, far, sample_gate, proj_weight, grad)
    hidden_grad, terms = grads(
        grad, gate_part, value_part, hidden, taps, grad_scale
    )
    terms, hidden_grad = order.after((terms, hidden_grad), ())
    received = swap(terms, 1)
    finish(0)
    hidden_grad = with_layout_constraint(
        jnp.transpose(hidden_grad, (1, 2, 0, 3)), Layout(major_to_minor=(0, 1, 2, 3))
    )
    hidden_grad = order.after(hidden_grad, ())
    finish(1)
    received = order.after(received, ())
    terms = order.after(terms + received, ())
    received = swap(terms, 2)
    received, far_sums[2] = order.after((received, far_sums[2]), ())
    others[0] = order.after(others[0], ())
    others[1] = order.after(others[1], ())
    finish(2)
    shape = (channels, depth)
    whole, conv_grad = put(
        order.token, mines, others[:2], firsts, shape, terms, received
    )
    bit = 4
    while bit < dp:
        conv_grad = conv_grad + swap(conv_grad, bit)
        bit *= 2
    whole, others[2] = order.after((whole, others[2]), ())
    column = firsts[2] + (1 - place[1]) * widths[2]
    whole = lax.dynamic_update_slice(whole, others[2], (0, column))
    return (hidden_grad[None], whole, conv_grad)


def solution(mesh):
    in_specs = (
        P("dp", None, None, None, "tensor"),
        P(None, None, None, "tensor"),
        P("tensor", None),
        P("dp", "tensor", None, None),
        P("dp", None),
    )
    out_specs = (
        P("dp", None, None, None, "tensor"),
        P("tensor", None),
        P(None, None, None, "tensor"),
    )
    return jax.shard_map(
        on_device, mesh=mesh, in_specs=in_specs, out_specs=out_specs, check_vma=False
    )
```

```python
import functools
import math

import jax
import jax.numpy as jnp
from jax import lax
from jax.experimental import pallas as pl
from jax.experimental.layout import Layout, with_layout_constraint
from jax.experimental.pallas import tpu as pltpu
from jax.sharding import PartitionSpec as P

F32 = jnp.float32
BF16 = jnp.bfloat16
PAD = 8
TILE = 16
LANES = 128
VMEM_BYTES = 20 * 1024 * 1024
VMEM = pl.BlockSpec(memory_space=pltpu.VMEM)


def ring_order(n):
    return [2 * i if i < n // 2 else 2 * (n - 1 - i) + 1 for i in range(n)]


def at_ring(position, n):
    position = lax.rem(position + 2 * n, n)
    return jnp.where(position < n // 2, 2 * position, 2 * (n - 1 - position) + 1)


def this_core():
    return lax.rem(lax.axis_index("dp"), 2)


def ring_place(index, n):
    half = index // 2
    return jnp.where(lax.rem(index, 2) == 0, half, n - 1 - half)


def params(limit=VMEM_BYTES):
    return pltpu.CompilerParams(vmem_limit_bytes=limit)


def cost(flops, moved, transcendentals=0):
    return pl.CostEstimate(flops=1, bytes_accessed=1, transcendentals=0)


def clear_edges(pad_ref, height, across):
    lanes = pad_ref.shape[-1]
    for k in range(2):
        pad_ref[k, 0] = jnp.zeros(pad_ref.shape[2:], F32)
        pad_ref[k, height + 1] = jnp.zeros(pad_ref.shape[2:], F32)

        @pl.loop(0, height)
        def _(r):
            pad_ref[k, r + 1, 0:PAD] = jnp.zeros((PAD, lanes), F32)
            pad_ref[k, r + 1, PAD + across : 2 * PAD + across] = jnp.zeros((PAD, lanes), F32)


def conv_kernel(first, count, hidden_ref, weight_ref, *refs):
    gate_ref, value_ref, mixed_ref, pad_ref = refs[-4:]
    _, height, across, channels = hidden_ref.shape
    clear_edges(pad_ref, height, across)

    @pl.loop(first, first + count)
    def _(c):
        lanes = pl.ds(pl.multiple_of(c * LANES, LANES), LANES)

        @pl.loop(0, height)
        def _(r):
            for k in range(2):
                pad_ref[k, r + 1, PAD : PAD + across] = hidden_ref[k, r, :, lanes].astype(F32)

        weights = weight_ref[:, lanes]

        @pl.loop(0, height)
        def _(r):
            mixed = []
            for t in range(across // TILE):
                w = t * TILE
                parts = []
                for k in range(2):
                    total = None
                    for i in range(3):
                        for j in range(3):
                            view = pad_ref[k, r + i, PAD + w + j - 1 : PAD + w + j - 1 + TILE]
                            term = weights[(i * 3 + j) * 2 + k][None, :] * view
                            total = term if total is None else total + term
                    parts.append(total)
                value, gate = parts
                sig = 1.0 / (1.0 + jnp.exp(-gate))
                gated = gate * sig
                gate_ref[r, w : w + TILE, lanes] = gated.astype(BF16)
                value_ref[r, w : w + TILE, lanes] = (
                    value * sig * (1.0 + gate * (1.0 - sig))
                ).astype(BF16)
                mixed.append((value * gated).astype(BF16))
            tokens = pl.ds(pl.multiple_of(r * across, LANES), across)
            mixed_ref[lanes, tokens] = jnp.concatenate(mixed, axis=0).T


def conv_parts(hidden, weights, first, count, before=()):
    _, height, across, channels = hidden.shape
    return pl.pallas_call(
        functools.partial(conv_kernel, first, count),
        in_specs=[VMEM] * (2 + len(before)),
        out_specs=[VMEM] * 3,
        out_shape=[
            jax.ShapeDtypeStruct((height, across, channels), BF16),
            jax.ShapeDtypeStruct((height, across, channels), BF16),
            jax.ShapeDtypeStruct((channels, height * across), BF16),
        ],
        scratch_shapes=[pltpu.VMEM((2, height + 2, across + 2 * PAD, LANES), F32)],
        input_output_aliases={2 + k: k for k in range(len(before))},
        compiler_params=params(),
        cost_estimate=cost(1, 1),
    )(hidden, weights, *before)


def rows_kernel(n, parts, numbers, added, *refs):
    count = len(numbers)
    pieces, refs = refs[:parts], refs[parts:]
    gate_ref, weight_ref, mixed_ref = refs[:3]
    sums_ref, grad_ref, local_ref, side_ref = refs[-4:]
    before_ref = refs[3] if added else None
    across = local_ref.shape[0] // count
    depth = local_ref.shape[1]
    spot = ring_place(lax.axis_index("tensor"), n)
    starts = [
        pl.multiple_of(at_ring(spot + step, n) * across, LANES) for step in numbers
    ]
    base = 0
    for piece in pieces:
        for r in range(0, piece.shape[0], TILE):
            local_ref[base + r : base + r + TILE] = (
                piece[r : r + TILE].astype(F32) * gate_ref[...]
            ).astype(BF16)
        base += piece.shape[0]
    for k, start in enumerate(starts):
        side_ref[:, k * across : (k + 1) * across] = mixed_ref[:, pl.ds(start, across)]
    block = min(depth, 512)
    for c in range(0, depth, block):
        total = jnp.dot(
            side_ref[...], local_ref[:, c : c + block], preferred_element_type=F32
        )
        if added:
            total = total + before_ref[:, c : c + block]
        sums_ref[:, c : c + block] = total
    product = lax.dot_general(
        local_ref[...], weight_ref[...], (((1,), (1,)), ((), ())), preferred_element_type=F32
    )
    for k, start in enumerate(starts):
        grad_ref[pl.ds(start, across)] = product[k * across : (k + 1) * across]


def rows_parts(n, pieces, numbers, gate, weight, mixed, before=None):
    depth = pieces[0].shape[1]
    channels, tokens = mixed.shape
    count, across = len(numbers), tokens // n
    operands = [*pieces, gate, weight, mixed]
    aliases = {}
    if before is not None:
        aliases = {len(operands): 0, len(operands) + 1: 1}
        operands += before
    return pl.pallas_call(
        functools.partial(rows_kernel, n, len(pieces), numbers, before is not None),
        in_specs=[VMEM] * len(operands),
        out_specs=[VMEM] * 2,
        out_shape=[
            jax.ShapeDtypeStruct((channels, depth), F32),
            jax.ShapeDtypeStruct((tokens, channels), F32),
        ],
        scratch_shapes=[
            pltpu.VMEM((count * across, depth), BF16),
            pltpu.VMEM((channels, count * across), BF16),
        ],
        input_output_aliases=aliases,
        compiler_params=params(),
        cost_estimate=cost(4 * count * across * channels * depth, 0),
    )(*operands)


def far_kernel(n, firsts, up_ref, down_ref, gate_ref, mixed_ref, before_ref, *refs):
    outs, local_ref = refs[:-1], refs[-1]
    half = up_ref.shape[0]
    across = 2 * half
    width = local_ref.shape[1]
    core = this_core()
    start = pl.multiple_of(
        at_ring(ring_place(lax.axis_index("tensor"), n) + n // 2, n) * across, LANES
    )
    columns = slice(firsts[0], firsts[0] + width)
    for base, piece in ((0, up_ref), (half, down_ref)):
        for r in range(0, half, TILE):
            local_ref[base + r : base + r + TILE] = (
                piece[r : r + TILE, columns].astype(F32) * gate_ref[:, columns]
            ).astype(BF16)
    mixed = mixed_ref[:, pl.ds(start, across)]
    for u, first in enumerate(firsts):
        for out_ref, side in ((outs[2 * u], 1 - core), (outs[2 * u + 1], core)):
            part = out_ref.shape[1]
            column = first + side * part
            total = jnp.dot(
                mixed,
                local_ref[:, pl.ds(pl.multiple_of(column - firsts[0], LANES), part)],
                preferred_element_type=F32,
            )
            total = total + before_ref[:, pl.ds(pl.multiple_of(column, LANES), part)]
            out_ref[...] = total.astype(out_ref.dtype)


def far_parts(n, pieces, firsts, widths, gate, mixed, before):
    channels, tokens = mixed.shape
    shapes = []
    for width in widths:
        shapes.append(jax.ShapeDtypeStruct((channels, width), BF16))
        shapes.append(jax.ShapeDtypeStruct((channels, width), F32))
    return pl.pallas_call(
        functools.partial(far_kernel, n, firsts),
        in_specs=[VMEM] * 5,
        out_specs=[VMEM] * len(shapes),
        out_shape=shapes,
        scratch_shapes=[pltpu.VMEM((tokens // n, 2 * sum(widths)), BF16)],
        compiler_params=params(),
        cost_estimate=cost(1, 1),
    )(*pieces, gate, mixed, before)


def far_row_kernel(n, up_ref, down_ref, gate_ref, weight_ref, before_ref, grad_ref, local_ref):
    half = up_ref.shape[0]
    across = 2 * half
    start = pl.multiple_of(at_ring(ring_place(lax.axis_index("tensor"), n) + n // 2, n) * across, LANES)
    for base, piece in ((0, up_ref), (half, down_ref)):
        for r in range(0, half, TILE):
            local_ref[base + r : base + r + TILE] = (
                piece[r : r + TILE].astype(F32) * gate_ref[...]
            ).astype(BF16)
    grad_ref[pl.ds(start, across)] = lax.dot_general(
        local_ref[...], weight_ref[...], (((1,), (1,)), ((), ())), preferred_element_type=F32
    )


def far_row(n, pieces, gate, weight, before):
    tokens, channels = before.shape
    return pl.pallas_call(
        functools.partial(far_row_kernel, n),
        in_specs=[VMEM] * 5,
        out_specs=VMEM,
        out_shape=jax.ShapeDtypeStruct(before.shape, F32),
        scratch_shapes=[pltpu.VMEM((tokens // n, weight.shape[1]), BF16)],
        input_output_aliases={4: 0},
        compiler_params=params(),
        cost_estimate=cost(1, 1),
    )(*pieces, gate, weight, before)


def grads_kernel(
    scale, grad_ref, gate_ref, value_ref, hidden_ref, taps_ref, out_ref, term_ref, pad_ref
):
    _, height, across, channels = hidden_ref.shape
    clear_edges(pad_ref, height, across)

    @pl.loop(0, channels // LANES)
    def _(c):
        lanes = pl.ds(pl.multiple_of(c * LANES, LANES), LANES)

        @pl.loop(0, height)
        def _(r):
            grad = grad_ref[pl.ds(pl.multiple_of(r * across, across), across), lanes]
            for k, factor in enumerate((gate_ref, value_ref)):
                pad_ref[k, r + 1, PAD : PAD + across] = grad * factor[r, :, lanes].astype(F32)

        weights = taps_ref[:, lanes]
        for k in range(2):

            def row(r, sums):
                sums = list(sums)
                for t in range(across // TILE):
                    w = t * TILE
                    own = hidden_ref[k, r, w : w + TILE, lanes].astype(F32)
                    total = None
                    for i in range(3):
                        for j in range(3):
                            view = pad_ref[k, r + 2 - i, PAD + w + 1 - j : PAD + w + 1 - j + TILE]
                            term = weights[(i * 3 + j) * 2 + k][None, :] * view
                            total = term if total is None else total + term
                            both = view * own
                            sums[i * 3 + j] = sums[i * 3 + j] + (both[:8] + both[8:])
                    out_ref[k, r, w : w + TILE, lanes] = total.astype(BF16)
                return tuple(sums)

            sums = lax.fori_loop(0, height, row, tuple(jnp.zeros((8, LANES), F32) for _ in range(9)))
            for tap in range(9):
                term_ref[tap // 3, tap % 3, k : k + 1, lanes] = scale * jnp.sum(
                    sums[tap], axis=0, keepdims=True
                )


def grads(grad, gate_part, value_part, hidden, taps, scale):
    _, height, across, channels = hidden.shape
    size = height * across * channels
    return pl.pallas_call(
        functools.partial(grads_kernel, scale),
        in_specs=[VMEM] * 5,
        out_specs=[VMEM, VMEM],
        out_shape=[
            jax.ShapeDtypeStruct(hidden.shape, BF16),
            jax.ShapeDtypeStruct((3, 3, 2, channels), F32),
        ],
        scratch_shapes=[pltpu.VMEM((2, height + 2, across + 2 * PAD, LANES), F32)],
        compiler_params=params(),
        cost_estimate=cost(size * 80, size * 20),
    )(grad, gate_part, value_part, hidden, taps)


def put_kernel(firsts, given, *refs):
    count = len(firsts)
    one_ref, two_ref, _, out_ref, total_ref, shares_ref, sems, share_sems = refs[-8:]
    shares = [
        pltpu.make_async_copy(ref, shares_ref.at[k], share_sems.at[k])
        for k, ref in enumerate((one_ref, two_ref))
    ]
    for copy in shares:
        copy.start()
    copies = []
    for k in range(count + given):
        half = refs[k].shape[1]
        core = this_core() if k < count else 1 - this_core()
        columns = pl.ds(pl.multiple_of(firsts[k % count] + core * half, LANES), half)
        copies.append(pltpu.make_async_copy(refs[k], out_ref.at[:, columns], sems.at[k]))
    for copy in copies:
        copy.start()
    for copy in shares:
        copy.wait()
    shares_ref[2] = shares_ref[0] + shares_ref[1]
    total = pltpu.make_async_copy(shares_ref.at[2], total_ref, share_sems.at[2])
    total.start()
    for copy in copies:
        copy.wait()
    total.wait()


def put(token, mines, others, firsts, shape, one, two):
    hbm = pl.BlockSpec(memory_space=pl.ANY)
    arrays = [*mines, *others]
    return pl.pallas_call(
        functools.partial(put_kernel, firsts, len(others)),
        in_specs=[hbm] * (len(arrays) + 3),
        out_specs=[hbm, hbm],
        out_shape=[jax.ShapeDtypeStruct(shape, BF16), jax.ShapeDtypeStruct(one.shape, F32)],
        scratch_shapes=[
            pltpu.VMEM((3, *one.shape), F32),
            pltpu.SemaphoreType.DMA((len(arrays),)),
            pltpu.SemaphoreType.DMA((3,)),
        ],
        compiler_params=params(),
        cost_estimate=cost(1, 1),
    )(*arrays, one, two, token)


class Order:
    def __init__(self, token):
        self.token = token

    def after(self, values, waited):
        flat, tree = jax.tree.flatten((values, waited, self.token))
        values, _, self.token = jax.tree.unflatten(tree, lax.optimization_barrier(flat))
        return values


def swap(value, bit):
    n = lax.axis_size("dp")
    return lax.ppermute(value, "dp", [(i, i ^ bit) for i in range(n)])


def sum_far(value, received):
    dp = lax.axis_size("dp")
    value = value.astype(F32) + received.astype(F32)
    bit = 4
    while bit < dp:
        value = value.astype(BF16)
        value = value.astype(F32) + swap(value, bit).astype(F32)
        bit *= 2
    return value


def on_device(hidden_in, conv_weight, proj_weight, out_grad, sample_gate):
    samples, height, across, _, channels = hidden_in.shape
    depth = out_grad.shape[-1]
    n = lax.axis_size("tensor")
    dp = lax.axis_size("dp")
    assert samples == 1 and out_grad.shape[1] == 1 and n % 2 == 0
    assert dp >= 4 and dp & (dp - 1) == 0
    grad_scale = 1.0 / math.sqrt(dp * samples * height * across)
    place = jnp.stack([lax.axis_index("tensor"), lax.rem(lax.axis_index("dp"), 2)]).astype(
        jnp.int32
    )
    own = out_grad.reshape(across, depth)
    hidden = jnp.transpose(hidden_in.reshape(height, across, 2, channels), (2, 0, 1, 3))
    taps = conv_weight.astype(F32).reshape(18, channels)
    order = Order(place)
    ring = ring_order(n)
    right = [(ring[i], ring[(i + 1) % n]) for i in range(n)]
    left = [(ring[i], ring[(i - 1) % n]) for i in range(n)]
    last = n // 2

    def rows(pieces, numbers, before):
        return rows_parts(n, pieces, numbers, sample_gate, proj_weight, mixed, before)

    half = across // 2
    state = {("up", 0): own[:half], ("down", 1): own[half:], ("up", 1): own[half:], ("down", 0): own[:half]}
    pieces, numbers, before = [own], [0], None
    blocks = channels // LANES
    early = blocks - blocks // 4
    for stage in range(1, last + 1):
        arrived = {}
        for way, part in state:
            if stage == last and (way, part) not in (("up", 0), ("down", 1)):
                arrived[way, part] = order.after(state[way, part], ())
                continue
            if stage > 1:
                state[way, part] = order.after(state[way, part], ())
            arrived[way, part] = state[way, part]
            state[way, part] = lax.ppermute(state[way, part], "tensor", right if way == "up" else left)
        if stage > 1:
            pieces += [arrived[way, part] for way in ("up", "down") for part in (0, 1)]
            numbers += [1 - stage, stage - 1]
        if stage == 1:
            hidden = order.after(hidden, ())
            conv = order.after(conv_parts(hidden, taps, 0, early), ())
        else:
            if stage == 2 and early < blocks:
                conv = order.after(conv_parts(hidden, taps, early, blocks - early, conv), ())
            gate_part, value_part, mixed = conv
            before = order.after(rows(pieces, numbers, before), ())
            pieces, numbers = [], []
    far = list(order.after((state["up", 0], state["down", 1]), ()))
    sums, grad = before

    eighth = depth // 8
    widths = [2 * eighth // 2, 3 * eighth // 2, 3 * eighth // 2]
    firsts = [sum(widths[:u]) * 2 for u in range(len(widths))]
    pairs, far_sums, mines, others = [], [], [], []

    def begin(u):
        received = order.after(near[u], ())
        pairs.append(order.after((keeps[u] + received.astype(F32)).astype(BF16), ()))
        far_sums.append(swap(pairs[u], 2))

    def finish(u):
        received = order.after(far_sums[u], ())
        mine = (sum_far(pairs[u], received) * grad_scale).astype(BF16)
        mines.append(order.after(mine, ()))
        others.append(swap(mines[u], 1))

    near, keeps = [], []
    for units in (slice(0, 1), slice(1, None)):
        parts = far_parts(n, far, firsts[units], widths[units], sample_gate, mixed, sums)
        parts, sums = order.after((parts, sums), ())
        near += [swap(part, 1) for part in parts[::2]]
        keeps += parts[1::2]
    begin(0)
    begin(1)
    begin(2)
    grad = order.after(grad, ())
    grad = far_row(n, far, sample_gate, proj_weight, grad)
    hidden_grad, terms = grads(
        grad, gate_part, value_part, hidden, taps, grad_scale
    )
    terms, hidden_grad = order.after((terms, hidden_grad), ())
    received = swap(terms, 1)
    finish(0)
    hidden_grad = with_layout_constraint(
        jnp.transpose(hidden_grad, (1, 2, 0, 3)), Layout(major_to_minor=(0, 1, 2, 3))
    )
    hidden_grad = order.after(hidden_grad, ())
    finish(1)
    received = order.after(received, ())
    terms = order.after(terms + received, ())
    received = swap(terms, 2)
    received, far_sums[2] = order.after((received, far_sums[2]), ())
    others[0] = order.after(others[0], ())
    others[1] = order.after(others[1], ())
    finish(2)
    shape = (channels, depth)
    whole, conv_grad = put(
        order.token, mines, others[:2], firsts, shape, terms, received
    )
    bit = 4
    while bit < dp:
        conv_grad = conv_grad + swap(conv_grad, bit)
        bit *= 2
    whole, others[2] = order.after((whole, others[2]), ())
    column = firsts[2] + (1 - place[1]) * widths[2]
    whole = lax.dynamic_update_slice(whole, others[2], (0, column))
    return (hidden_grad[None], whole, conv_grad)


def solution(mesh):
    in_specs = (
        P("dp", None, None, None, "tensor"),
        P(None, None, None, "tensor"),
        P("tensor", None),
        P("dp", "tensor", None, None),
        P("dp", None),
    )
    out_specs = (
        P("dp", None, None, None, "tensor"),
        P("tensor", None),
        P(None, None, None, "tensor"),
    )
    return jax.shard_map(
        on_device, mesh=mesh, in_specs=in_specs, out_specs=out_specs, check_vma=False
    )
```

```python
import functools
import math

import jax
import jax.numpy as jnp
from jax import lax
from jax.experimental import pallas as pl
from jax.experimental.layout import Layout, with_layout_constraint
from jax.experimental.pallas import tpu as pltpu
from jax.sharding import PartitionSpec as P

F32 = jnp.float32
BF16 = jnp.bfloat16
PAD = 8
TILE = 16
LANES = 128
VMEM_BYTES = 20 * 1024 * 1024
VMEM = pl.BlockSpec(memory_space=pltpu.VMEM)


def ring_order(n):
    return [2 * i if i < n // 2 else 2 * (n - 1 - i) + 1 for i in range(n)]


def at_ring(position, n):
    position = lax.rem(position + 2 * n, n)
    return jnp.where(position < n // 2, 2 * position, 2 * (n - 1 - position) + 1)


def this_core():
    return lax.rem(lax.axis_index("dp"), 2)


def ring_place(index, n):
    half = index // 2
    return jnp.where(lax.rem(index, 2) == 0, half, n - 1 - half)


def params(limit=VMEM_BYTES):
    return pltpu.CompilerParams(vmem_limit_bytes=limit)


def cost(flops, moved, transcendentals=0):
    return pl.CostEstimate(flops=1, bytes_accessed=1, transcendentals=0)


def clear_edges(pad_ref, height, across):
    lanes = pad_ref.shape[-1]
    for k in range(2):
        pad_ref[k, 0] = jnp.zeros(pad_ref.shape[2:], F32)
        pad_ref[k, height + 1] = jnp.zeros(pad_ref.shape[2:], F32)

        @pl.loop(0, height)
        def _(r):
            pad_ref[k, r + 1, 0:PAD] = jnp.zeros((PAD, lanes), F32)
            pad_ref[k, r + 1, PAD + across : 2 * PAD + across] = jnp.zeros((PAD, lanes), F32)


def conv_kernel(first, count, hidden_ref, weight_ref, *refs):
    gate_ref, value_ref, mixed_ref, pad_ref = refs[-4:]
    _, height, across, channels = hidden_ref.shape
    clear_edges(pad_ref, height, across)

    @pl.loop(first, first + count)
    def _(c):
        lanes = pl.ds(pl.multiple_of(c * LANES, LANES), LANES)

        @pl.loop(0, height)
        def _(r):
            for k in range(2):
                pad_ref[k, r + 1, PAD : PAD + across] = hidden_ref[k, r, :, lanes].astype(F32)

        weights = weight_ref[:, lanes]

        @pl.loop(0, height)
        def _(r):
            mixed = []
            for t in range(across // TILE):
                w = t * TILE
                parts = []
                for k in range(2):
                    total = None
                    for i in range(3):
                        for j in range(3):
                            view = pad_ref[k, r + i, PAD + w + j - 1 : PAD + w + j - 1 + TILE]
                            term = weights[(i * 3 + j) * 2 + k][None, :] * view
                            total = term if total is None else total + term
                    parts.append(total)
                value, gate = parts
                sig = 1.0 / (1.0 + jnp.exp(-gate))
                gated = gate * sig
                gate_ref[r, w : w + TILE, lanes] = gated.astype(BF16)
                value_ref[r, w : w + TILE, lanes] = (
                    value * sig * (1.0 + gate * (1.0 - sig))
                ).astype(BF16)
                mixed.append((value * gated).astype(BF16))
            tokens = pl.ds(pl.multiple_of(r * across, LANES), across)
            mixed_ref[lanes, tokens] = jnp.concatenate(mixed, axis=0).T


def conv_parts(hidden, weights, first, count, before=()):
    _, height, across, channels = hidden.shape
    return pl.pallas_call(
        functools.partial(conv_kernel, first, count),
        in_specs=[VMEM] * (2 + len(before)),
        out_specs=[VMEM] * 3,
        out_shape=[
            jax.ShapeDtypeStruct((height, across, channels), BF16),
            jax.ShapeDtypeStruct((height, across, channels), BF16),
            jax.ShapeDtypeStruct((channels, height * across), BF16),
        ],
        scratch_shapes=[pltpu.VMEM((2, height + 2, across + 2 * PAD, LANES), F32)],
        input_output_aliases={2 + k: k for k in range(len(before))},
        compiler_params=params(),
        cost_estimate=cost(1, 1),
    )(hidden, weights, *before)


def rows_kernel(n, parts, numbers, added, *refs):
    count = len(numbers)
    pieces, refs = refs[:parts], refs[parts:]
    gate_ref, weight_ref, mixed_ref = refs[:3]
    sums_ref, grad_ref, local_ref, side_ref = refs[-4:]
    before_ref = refs[3] if added else None
    across = local_ref.shape[0] // count
    depth = local_ref.shape[1]
    spot = ring_place(lax.axis_index("tensor"), n)
    starts = [
        pl.multiple_of(at_ring(spot + step, n) * across, LANES) for step in numbers
    ]
    base = 0
    for piece in pieces:
        for r in range(0, piece.shape[0], TILE):
            local_ref[base + r : base + r + TILE] = (
                piece[r : r + TILE].astype(F32) * gate_ref[...]
            ).astype(BF16)
        base += piece.shape[0]
    for k, start in enumerate(starts):
        side_ref[:, k * across : (k + 1) * across] = mixed_ref[:, pl.ds(start, across)]
    block = min(depth, 512)
    for c in range(0, depth, block):
        total = jnp.dot(
            side_ref[...], local_ref[:, c : c + block], preferred_element_type=F32
        )
        if added:
            total = total + before_ref[:, c : c + block]
        sums_ref[:, c : c + block] = total
    product = lax.dot_general(
        local_ref[...], weight_ref[...], (((1,), (1,)), ((), ())), preferred_element_type=F32
    )
    for k, start in enumerate(starts):
        grad_ref[pl.ds(start, across)] = product[k * across : (k + 1) * across]


def rows_parts(n, pieces, numbers, gate, weight, mixed, before=None):
    depth = pieces[0].shape[1]
    channels, tokens = mixed.shape
    count, across = len(numbers), tokens // n
    operands = [*pieces, gate, weight, mixed]
    aliases = {}
    if before is not None:
        aliases = {len(operands): 0, len(operands) + 1: 1}
        operands += before
    return pl.pallas_call(
        functools.partial(rows_kernel, n, len(pieces), numbers, before is not None),
        in_specs=[VMEM] * len(operands),
        out_specs=[VMEM] * 2,
        out_shape=[
            jax.ShapeDtypeStruct((channels, depth), F32),
            jax.ShapeDtypeStruct((tokens, channels), F32),
        ],
        scratch_shapes=[
            pltpu.VMEM((count * across, depth), BF16),
            pltpu.VMEM((channels, count * across), BF16),
        ],
        input_output_aliases=aliases,
        compiler_params=params(),
        cost_estimate=cost(4 * count * across * channels * depth, 0),
    )(*operands)


def far_kernel(n, firsts, up_ref, down_ref, gate_ref, mixed_ref, before_ref, *refs):
    outs, local_ref = refs[:-1], refs[-1]
    half = up_ref.shape[0]
    across = 2 * half
    width = local_ref.shape[1]
    core = this_core()
    start = pl.multiple_of(
        at_ring(ring_place(lax.axis_index("tensor"), n) + n // 2, n) * across, LANES
    )
    columns = slice(firsts[0], firsts[0] + width)
    for base, piece in ((0, up_ref), (half, down_ref)):
        for r in range(0, half, TILE):
            local_ref[base + r : base + r + TILE] = (
                piece[r : r + TILE, columns].astype(F32) * gate_ref[:, columns]
            ).astype(BF16)
    mixed = mixed_ref[:, pl.ds(start, across)]
    for u, first in enumerate(firsts):
        for out_ref, side in ((outs[2 * u], 1 - core), (outs[2 * u + 1], core)):
            part = out_ref.shape[1]
            column = first + side * part
            total = jnp.dot(
                mixed,
                local_ref[:, pl.ds(pl.multiple_of(column - firsts[0], LANES), part)],
                preferred_element_type=F32,
            )
            total = total + before_ref[:, pl.ds(pl.multiple_of(column, LANES), part)]
            out_ref[...] = total.astype(out_ref.dtype)


def far_parts(n, pieces, firsts, widths, gate, mixed, before):
    channels, tokens = mixed.shape
    shapes = []
    for width in widths:
        shapes.append(jax.ShapeDtypeStruct((channels, width), BF16))
        shapes.append(jax.ShapeDtypeStruct((channels, width), F32))
    return pl.pallas_call(
        functools.partial(far_kernel, n, firsts),
        in_specs=[VMEM] * 5,
        out_specs=[VMEM] * len(shapes),
        out_shape=shapes,
        scratch_shapes=[pltpu.VMEM((tokens // n, 2 * sum(widths)), BF16)],
        compiler_params=params(),
        cost_estimate=cost(1, 1),
    )(*pieces, gate, mixed, before)


def far_row_kernel(n, up_ref, down_ref, gate_ref, weight_ref, before_ref, grad_ref, local_ref):
    half = up_ref.shape[0]
    across = 2 * half
    start = pl.multiple_of(at_ring(ring_place(lax.axis_index("tensor"), n) + n // 2, n) * across, LANES)
    for base, piece in ((0, up_ref), (half, down_ref)):
        for r in range(0, half, TILE):
            local_ref[base + r : base + r + TILE] = (
                piece[r : r + TILE].astype(F32) * gate_ref[...]
            ).astype(BF16)
    grad_ref[pl.ds(start, across)] = lax.dot_general(
        local_ref[...], weight_ref[...], (((1,), (1,)), ((), ())), preferred_element_type=F32
    )


def far_row(n, pieces, gate, weight, before):
    tokens, channels = before.shape
    return pl.pallas_call(
        functools.partial(far_row_kernel, n),
        in_specs=[VMEM] * 5,
        out_specs=VMEM,
        out_shape=jax.ShapeDtypeStruct(before.shape, F32),
        scratch_shapes=[pltpu.VMEM((tokens // n, weight.shape[1]), BF16)],
        input_output_aliases={4: 0},
        compiler_params=params(),
        cost_estimate=cost(1, 1),
    )(*pieces, gate, weight, before)


def grads_kernel(
    scale, grad_ref, gate_ref, value_ref, hidden_ref, taps_ref, out_ref, term_ref, pad_ref
):
    _, height, across, channels = hidden_ref.shape
    clear_edges(pad_ref, height, across)

    @pl.loop(0, channels // LANES)
    def _(c):
        lanes = pl.ds(pl.multiple_of(c * LANES, LANES), LANES)

        @pl.loop(0, height)
        def _(r):
            grad = grad_ref[pl.ds(pl.multiple_of(r * across, across), across), lanes]
            for k, factor in enumerate((gate_ref, value_ref)):
                pad_ref[k, r + 1, PAD : PAD + across] = grad * factor[r, :, lanes].astype(F32)

        weights = taps_ref[:, lanes]
        for k in range(2):

            def row(r, sums):
                sums = list(sums)
                for t in range(across // TILE):
                    w = t * TILE
                    own = hidden_ref[k, r, w : w + TILE, lanes].astype(F32)
                    total = None
                    for i in range(3):
                        for j in range(3):
                            view = pad_ref[k, r + 2 - i, PAD + w + 1 - j : PAD + w + 1 - j + TILE]
                            term = weights[(i * 3 + j) * 2 + k][None, :] * view
                            total = term if total is None else total + term
                            both = view * own
                            sums[i * 3 + j] = sums[i * 3 + j] + (both[:8] + both[8:])
                    out_ref[k, r, w : w + TILE, lanes] = total.astype(BF16)
                return tuple(sums)

            sums = lax.fori_loop(0, height, row, tuple(jnp.zeros((8, LANES), F32) for _ in range(9)))
            for tap in range(9):
                term_ref[tap // 3, tap % 3, k : k + 1, lanes] = scale * jnp.sum(
                    sums[tap], axis=0, keepdims=True
                )


def grads(grad, gate_part, value_part, hidden, taps, scale):
    _, height, across, channels = hidden.shape
    size = height * across * channels
    return pl.pallas_call(
        functools.partial(grads_kernel, scale),
        in_specs=[VMEM] * 5,
        out_specs=[VMEM, VMEM],
        out_shape=[
            jax.ShapeDtypeStruct(hidden.shape, BF16),
            jax.ShapeDtypeStruct((3, 3, 2, channels), F32),
        ],
        scratch_shapes=[pltpu.VMEM((2, height + 2, across + 2 * PAD, LANES), F32)],
        compiler_params=params(),
        cost_estimate=cost(size * 80, size * 20),
    )(grad, gate_part, value_part, hidden, taps)


def put_kernel(firsts, given, *refs):
    count = len(firsts)
    one_ref, two_ref, _, out_ref, total_ref, shares_ref, sems, share_sems = refs[-8:]
    shares = [
        pltpu.make_async_copy(ref, shares_ref.at[k], share_sems.at[k])
        for k, ref in enumerate((one_ref, two_ref))
    ]
    for copy in shares:
        copy.start()
    copies = []
    for k in range(count + given):
        half = refs[k].shape[1]
        core = this_core() if k < count else 1 - this_core()
        columns = pl.ds(pl.multiple_of(firsts[k % count] + core * half, LANES), half)
        copies.append(pltpu.make_async_copy(refs[k], out_ref.at[:, columns], sems.at[k]))
    for copy in copies:
        copy.start()
    for copy in shares:
        copy.wait()
    shares_ref[2] = shares_ref[0] + shares_ref[1]
    total = pltpu.make_async_copy(shares_ref.at[2], total_ref, share_sems.at[2])
    total.start()
    for copy in copies:
        copy.wait()
    total.wait()


def put(token, mines, others, firsts, shape, one, two):
    hbm = pl.BlockSpec(memory_space=pl.ANY)
    arrays = [*mines, *others]
    return pl.pallas_call(
        functools.partial(put_kernel, firsts, len(others)),
        in_specs=[hbm] * (len(arrays) + 3),
        out_specs=[hbm, hbm],
        out_shape=[jax.ShapeDtypeStruct(shape, BF16), jax.ShapeDtypeStruct(one.shape, F32)],
        scratch_shapes=[
            pltpu.VMEM((3, *one.shape), F32),
            pltpu.SemaphoreType.DMA((len(arrays),)),
            pltpu.SemaphoreType.DMA((3,)),
        ],
        compiler_params=params(),
        cost_estimate=cost(1, 1),
    )(*arrays, one, two, token)


class Order:
    def __init__(self, token):
        self.token = token

    def after(self, values, waited):
        flat, tree = jax.tree.flatten((values, waited, self.token))
        values, _, self.token = jax.tree.unflatten(tree, lax.optimization_barrier(flat))
        return values


def swap(value, bit):
    n = lax.axis_size("dp")
    return lax.ppermute(value, "dp", [(i, i ^ bit) for i in range(n)])


def sum_far(value, received):
    dp = lax.axis_size("dp")
    value = value.astype(F32) + received.astype(F32)
    bit = 4
    while bit < dp:
        value = value.astype(BF16)
        value = value.astype(F32) + swap(value, bit).astype(F32)
        bit *= 2
    return value


def on_device(hidden_in, conv_weight, proj_weight, out_grad, sample_gate):
    samples, height, across, _, channels = hidden_in.shape
    depth = out_grad.shape[-1]
    n = lax.axis_size("tensor")
    dp = lax.axis_size("dp")
    assert samples == 1 and out_grad.shape[1] == 1 and n % 2 == 0
    assert dp >= 4 and dp & (dp - 1) == 0
    grad_scale = 1.0 / math.sqrt(dp * samples * height * across)
    place = jnp.stack([lax.axis_index("tensor"), lax.rem(lax.axis_index("dp"), 2)]).astype(
        jnp.int32
    )
    own = out_grad.reshape(across, depth)
    hidden = jnp.transpose(hidden_in.reshape(height, across, 2, channels), (2, 0, 1, 3))
    taps = conv_weight.astype(F32).reshape(18, channels)
    order = Order(place)
    ring = ring_order(n)
    right = [(ring[i], ring[(i + 1) % n]) for i in range(n)]
    left = [(ring[i], ring[(i - 1) % n]) for i in range(n)]
    last = n // 2

    def rows(pieces, numbers, before):
        return rows_parts(n, pieces, numbers, sample_gate, proj_weight, mixed, before)

    half = across // 2
    state = {("up", 0): own[:half], ("down", 1): own[half:], ("up", 1): own[half:], ("down", 0): own[:half]}
    pieces, numbers, before = [own], [0], None
    blocks = channels // LANES
    early = blocks - blocks // 4
    for stage in range(1, last + 1):
        arrived = {}
        for way, part in state:
            if stage == last and (way, part) not in (("up", 0), ("down", 1)):
                arrived[way, part] = order.after(state[way, part], ())
                continue
            if stage > 1:
                state[way, part] = order.after(state[way, part], ())
            arrived[way, part] = state[way, part]
            state[way, part] = lax.ppermute(state[way, part], "tensor", right if way == "up" else left)
        if stage > 1:
            pieces += [arrived[way, part] for way in ("up", "down") for part in (0, 1)]
            numbers += [1 - stage, stage - 1]
        if stage == 1:
            hidden = order.after(hidden, ())
            conv = order.after(conv_parts(hidden, taps, 0, early), ())
        else:
            if stage == 2 and early < blocks:
                conv = order.after(conv_parts(hidden, taps, early, blocks - early, conv), ())
            gate_part, value_part, mixed = conv
            before = order.after(rows(pieces, numbers, before), ())
            pieces, numbers = [], []
    far = list(order.after((state["up", 0], state["down", 1]), ()))
    sums, grad = before

    eighth = depth // 8
    widths = [2 * eighth // 2, 3 * eighth // 2, 3 * eighth // 2]
    firsts = [sum(widths[:u]) * 2 for u in range(len(widths))]
    pairs, far_sums, mines, others = [], [], [], []

    def begin(u):
        received = order.after(near[u], ())
        pairs.append(order.after((keeps[u] + received.astype(F32)).astype(BF16), ()))
        far_sums.append(swap(pairs[u], 2))

    def finish(u):
        received = order.after(far_sums[u], ())
        mine = (sum_far(pairs[u], received) * grad_scale).astype(BF16)
        mines.append(order.after(mine, ()))
        others.append(swap(mines[u], 1))

    near, keeps = [], []
    for units in (slice(0, 1), slice(1, None)):
        parts = far_parts(n, far, firsts[units], widths[units], sample_gate, mixed, sums)
        parts, sums = order.after((parts, sums), ())
        near += [swap(part, 1) for part in parts[::2]]
        keeps += parts[1::2]
    begin(0)
    begin(1)
    begin(2)
    grad = order.after(grad, ())
    grad = far_row(n, far, sample_gate, proj_weight, grad)
    hidden_grad, terms = grads(
        grad, gate_part, value_part, hidden, taps, grad_scale
    )
    terms, hidden_grad = order.after((terms, hidden_grad), ())
    received = swap(terms, 1)
    finish(0)
    hidden_grad = with_layout_constraint(
        jnp.transpose(hidden_grad, (1, 2, 0, 3)), Layout(major_to_minor=(0, 1, 2, 3))
    )
    hidden_grad = order.after(hidden_grad, ())
    finish(1)
    received = order.after(received, ())
    terms = order.after((terms + received).astype(BF16), ())
    received = swap(terms, 2)
    received, far_sums[2] = order.after((received, far_sums[2]), ())
    others[0] = order.after(others[0], ())
    others[1] = order.after(others[1], ())
    finish(2)
    shape = (channels, depth)
    whole, conv_grad = put(
        order.token, mines, others[:2], firsts, shape, terms.astype(F32), received.astype(F32)
    )
    bit = 4
    while bit < dp:
        conv_grad = conv_grad + swap(conv_grad, bit)
        bit *= 2
    whole, others[2] = order.after((whole, others[2]), ())
    column = firsts[2] + (1 - place[1]) * widths[2]
    whole = lax.dynamic_update_slice(whole, others[2], (0, column))
    return (hidden_grad[None], whole, conv_grad)


def solution(mesh):
    in_specs = (
        P("dp", None, None, None, "tensor"),
        P(None, None, None, "tensor"),
        P("tensor", None),
        P("dp", "tensor", None, None),
        P("dp", None),
    )
    out_specs = (
        P("dp", None, None, None, "tensor"),
        P("tensor", None),
        P(None, None, None, "tensor"),
    )
    return jax.shard_map(
        on_device, mesh=mesh, in_specs=in_specs, out_specs=out_specs, check_vma=False
    )
```

```python
import functools
import math

import jax
import jax.numpy as jnp
from jax import lax
from jax.experimental import pallas as pl
from jax.experimental.layout import Layout, with_layout_constraint
from jax.experimental.pallas import tpu as pltpu
from jax.sharding import PartitionSpec as P

F32 = jnp.float32
BF16 = jnp.bfloat16
PAD = 8
TILE = 16
LANES = 128
VMEM_BYTES = 20 * 1024 * 1024
VMEM = pl.BlockSpec(memory_space=pltpu.VMEM)


def ring_order(n):
    return [2 * i if i < n // 2 else 2 * (n - 1 - i) + 1 for i in range(n)]


def at_ring(position, n):
    position = lax.rem(position + 2 * n, n)
    return jnp.where(position < n // 2, 2 * position, 2 * (n - 1 - position) + 1)


def this_core():
    return lax.rem(lax.axis_index("dp"), 2)


def ring_place(index, n):
    half = index // 2
    return jnp.where(lax.rem(index, 2) == 0, half, n - 1 - half)


def params(limit=VMEM_BYTES):
    return pltpu.CompilerParams(vmem_limit_bytes=limit)


def cost(flops, moved, transcendentals=0):
    return pl.CostEstimate(flops=1, bytes_accessed=1, transcendentals=0)


def clear_edges(pad_ref, height, across):
    lanes = pad_ref.shape[-1]
    for k in range(2):
        pad_ref[k, 0] = jnp.zeros(pad_ref.shape[2:], F32)
        pad_ref[k, height + 1] = jnp.zeros(pad_ref.shape[2:], F32)

        @pl.loop(0, height)
        def _(r):
            pad_ref[k, r + 1, 0:PAD] = jnp.zeros((PAD, lanes), F32)
            pad_ref[k, r + 1, PAD + across : 2 * PAD + across] = jnp.zeros((PAD, lanes), F32)


def conv_kernel(first, count, hidden_ref, weight_ref, *refs):
    gate_ref, value_ref, mixed_ref, pad_ref = refs[-4:]
    _, height, across, channels = hidden_ref.shape
    clear_edges(pad_ref, height, across)

    @pl.loop(first, first + count)
    def _(c):
        lanes = pl.ds(pl.multiple_of(c * LANES, LANES), LANES)

        @pl.loop(0, height)
        def _(r):
            for k in range(2):
                pad_ref[k, r + 1, PAD : PAD + across] = hidden_ref[k, r, :, lanes].astype(F32)

        weights = weight_ref[:, lanes]

        @pl.loop(0, height)
        def _(r):
            mixed = []
            for t in range(across // TILE):
                w = t * TILE
                parts = []
                for k in range(2):
                    total = None
                    for i in range(3):
                        for j in range(3):
                            view = pad_ref[k, r + i, PAD + w + j - 1 : PAD + w + j - 1 + TILE]
                            term = weights[(i * 3 + j) * 2 + k][None, :] * view
                            total = term if total is None else total + term
                    parts.append(total)
                value, gate = parts
                sig = 1.0 / (1.0 + jnp.exp(-gate))
                gated = gate * sig
                gate_ref[r, w : w + TILE, lanes] = gated.astype(BF16)
                value_ref[r, w : w + TILE, lanes] = (
                    value * sig * (1.0 + gate * (1.0 - sig))
                ).astype(BF16)
                mixed.append((value * gated).astype(BF16))
            tokens = pl.ds(pl.multiple_of(r * across, LANES), across)
            mixed_ref[lanes, tokens] = jnp.concatenate(mixed, axis=0).T


def conv_parts(hidden, weights, first, count, before=()):
    _, height, across, channels = hidden.shape
    return pl.pallas_call(
        functools.partial(conv_kernel, first, count),
        in_specs=[VMEM] * (2 + len(before)),
        out_specs=[VMEM] * 3,
        out_shape=[
            jax.ShapeDtypeStruct((height, across, channels), BF16),
            jax.ShapeDtypeStruct((height, across, channels), BF16),
            jax.ShapeDtypeStruct((channels, height * across), BF16),
        ],
        scratch_shapes=[pltpu.VMEM((2, height + 2, across + 2 * PAD, LANES), F32)],
        input_output_aliases={2 + k: k for k in range(len(before))},
        compiler_params=params(),
        cost_estimate=cost(1, 1),
    )(hidden, weights, *before)


def rows_kernel(n, parts, numbers, added, *refs):
    count = len(numbers)
    pieces, refs = refs[:parts], refs[parts:]
    gate_ref, weight_ref, mixed_ref = refs[:3]
    sums_ref, grad_ref, local_ref, side_ref = refs[-4:]
    before_ref = refs[3] if added else None
    across = local_ref.shape[0] // count
    depth = local_ref.shape[1]
    spot = ring_place(lax.axis_index("tensor"), n)
    starts = [
        pl.multiple_of(at_ring(spot + step, n) * across, LANES) for step in numbers
    ]
    base = 0
    for piece in pieces:
        for r in range(0, piece.shape[0], TILE):
            local_ref[base + r : base + r + TILE] = (
                piece[r : r + TILE].astype(F32) * gate_ref[...]
            ).astype(BF16)
        base += piece.shape[0]
    for k, start in enumerate(starts):
        side_ref[:, k * across : (k + 1) * across] = mixed_ref[:, pl.ds(start, across)]
    block = min(depth, 512)
    for c in range(0, depth, block):
        total = jnp.dot(
            side_ref[...], local_ref[:, c : c + block], preferred_element_type=F32
        )
        if added:
            total = total + before_ref[:, c : c + block]
        sums_ref[:, c : c + block] = total
    product = lax.dot_general(
        local_ref[...], weight_ref[...], (((1,), (1,)), ((), ())), preferred_element_type=F32
    )
    for k, start in enumerate(starts):
        grad_ref[pl.ds(start, across)] = product[k * across : (k + 1) * across]


def rows_parts(n, pieces, numbers, gate, weight, mixed, before=None):
    depth = pieces[0].shape[1]
    channels, tokens = mixed.shape
    count, across = len(numbers), tokens // n
    operands = [*pieces, gate, weight, mixed]
    aliases = {}
    if before is not None:
        aliases = {len(operands): 0, len(operands) + 1: 1}
        operands += before
    return pl.pallas_call(
        functools.partial(rows_kernel, n, len(pieces), numbers, before is not None),
        in_specs=[VMEM] * len(operands),
        out_specs=[VMEM] * 2,
        out_shape=[
            jax.ShapeDtypeStruct((channels, depth), F32),
            jax.ShapeDtypeStruct((tokens, channels), F32),
        ],
        scratch_shapes=[
            pltpu.VMEM((count * across, depth), BF16),
            pltpu.VMEM((channels, count * across), BF16),
        ],
        input_output_aliases=aliases,
        compiler_params=params(),
        cost_estimate=cost(4 * count * across * channels * depth, 0),
    )(*operands)


def far_kernel(n, firsts, up_ref, down_ref, gate_ref, mixed_ref, before_ref, *refs):
    outs, local_ref = refs[:-1], refs[-1]
    half = up_ref.shape[0]
    across = 2 * half
    width = local_ref.shape[1]
    core = this_core()
    start = pl.multiple_of(
        at_ring(ring_place(lax.axis_index("tensor"), n) + n // 2, n) * across, LANES
    )
    columns = slice(firsts[0], firsts[0] + width)
    for base, piece in ((0, up_ref), (half, down_ref)):
        for r in range(0, half, TILE):
            local_ref[base + r : base + r + TILE] = (
                piece[r : r + TILE, columns].astype(F32) * gate_ref[:, columns]
            ).astype(BF16)
    mixed = mixed_ref[:, pl.ds(start, across)]
    for u, first in enumerate(firsts):
        for out_ref, side in ((outs[2 * u], 1 - core), (outs[2 * u + 1], core)):
            part = out_ref.shape[1]
            column = first + side * part
            total = jnp.dot(
                mixed,
                local_ref[:, pl.ds(pl.multiple_of(column - firsts[0], LANES), part)],
                preferred_element_type=F32,
            )
            total = total + before_ref[:, pl.ds(pl.multiple_of(column, LANES), part)]
            out_ref[...] = total.astype(out_ref.dtype)


def far_parts(n, pieces, firsts, widths, gate, mixed, before):
    channels, tokens = mixed.shape
    shapes = []
    for width in widths:
        shapes.append(jax.ShapeDtypeStruct((channels, width), BF16))
        shapes.append(jax.ShapeDtypeStruct((channels, width), F32))
    return pl.pallas_call(
        functools.partial(far_kernel, n, firsts),
        in_specs=[VMEM] * 5,
        out_specs=[VMEM] * len(shapes),
        out_shape=shapes,
        scratch_shapes=[pltpu.VMEM((tokens // n, 2 * sum(widths)), BF16)],
        compiler_params=params(),
        cost_estimate=cost(1, 1),
    )(*pieces, gate, mixed, before)


def far_row_kernel(n, up_ref, down_ref, gate_ref, weight_ref, before_ref, grad_ref, local_ref):
    half = up_ref.shape[0]
    across = 2 * half
    start = pl.multiple_of(at_ring(ring_place(lax.axis_index("tensor"), n) + n // 2, n) * across, LANES)
    for base, piece in ((0, up_ref), (half, down_ref)):
        for r in range(0, half, TILE):
            local_ref[base + r : base + r + TILE] = (
                piece[r : r + TILE].astype(F32) * gate_ref[...]
            ).astype(BF16)
    grad_ref[pl.ds(start, across)] = lax.dot_general(
        local_ref[...], weight_ref[...], (((1,), (1,)), ((), ())), preferred_element_type=F32
    )


def far_row(n, pieces, gate, weight, before):
    tokens, channels = before.shape
    return pl.pallas_call(
        functools.partial(far_row_kernel, n),
        in_specs=[VMEM] * 5,
        out_specs=VMEM,
        out_shape=jax.ShapeDtypeStruct(before.shape, F32),
        scratch_shapes=[pltpu.VMEM((tokens // n, weight.shape[1]), BF16)],
        input_output_aliases={4: 0},
        compiler_params=params(),
        cost_estimate=cost(1, 1),
    )(*pieces, gate, weight, before)


def grads_kernel(
    scale, grad_ref, gate_ref, value_ref, hidden_ref, taps_ref, out_ref, term_ref, pad_ref
):
    _, height, across, channels = hidden_ref.shape
    clear_edges(pad_ref, height, across)

    @pl.loop(0, channels // LANES)
    def _(c):
        lanes = pl.ds(pl.multiple_of(c * LANES, LANES), LANES)

        @pl.loop(0, height)
        def _(r):
            grad = grad_ref[pl.ds(pl.multiple_of(r * across, across), across), lanes]
            for k, factor in enumerate((gate_ref, value_ref)):
                pad_ref[k, r + 1, PAD : PAD + across] = grad * factor[r, :, lanes].astype(F32)

        weights = taps_ref[:, lanes]
        for k in range(2):

            def row(r, sums):
                sums = list(sums)
                for t in range(across // TILE):
                    w = t * TILE
                    own = hidden_ref[k, r, w : w + TILE, lanes].astype(F32)
                    total = None
                    for i in range(3):
                        for j in range(3):
                            view = pad_ref[k, r + 2 - i, PAD + w + 1 - j : PAD + w + 1 - j + TILE]
                            term = weights[(i * 3 + j) * 2 + k][None, :] * view
                            total = term if total is None else total + term
                            both = view * own
                            sums[i * 3 + j] = sums[i * 3 + j] + (both[:8] + both[8:])
                    out_ref[k, r, w : w + TILE, lanes] = total.astype(BF16)
                return tuple(sums)

            sums = lax.fori_loop(0, height, row, tuple(jnp.zeros((8, LANES), F32) for _ in range(9)))
            for tap in range(9):
                term_ref[tap // 3, tap % 3, k : k + 1, lanes] = scale * jnp.sum(
                    sums[tap], axis=0, keepdims=True
                )


def grads(grad, gate_part, value_part, hidden, taps, scale):
    _, height, across, channels = hidden.shape
    size = height * across * channels
    return pl.pallas_call(
        functools.partial(grads_kernel, scale),
        in_specs=[VMEM] * 5,
        out_specs=[VMEM, VMEM],
        out_shape=[
            jax.ShapeDtypeStruct(hidden.shape, BF16),
            jax.ShapeDtypeStruct((3, 3, 2, channels), F32),
        ],
        scratch_shapes=[pltpu.VMEM((2, height + 2, across + 2 * PAD, LANES), F32)],
        compiler_params=params(),
        cost_estimate=cost(size * 80, size * 20),
    )(grad, gate_part, value_part, hidden, taps)


def put_kernel(firsts, given, *refs):
    count = len(firsts)
    one_ref, two_ref, _, out_ref, total_ref, shares_ref, sems, share_sems = refs[-8:]
    shares = [
        pltpu.make_async_copy(ref, shares_ref.at[k], share_sems.at[k])
        for k, ref in enumerate((one_ref, two_ref))
    ]
    for copy in shares:
        copy.start()
    copies = []
    for k in range(count + given):
        half = refs[k].shape[1]
        core = this_core() if k < count else 1 - this_core()
        columns = pl.ds(pl.multiple_of(firsts[k % count] + core * half, LANES), half)
        copies.append(pltpu.make_async_copy(refs[k], out_ref.at[:, columns], sems.at[k]))
    for copy in copies:
        copy.start()
    for copy in shares:
        copy.wait()
    shares_ref[2] = shares_ref[0] + shares_ref[1]
    total = pltpu.make_async_copy(shares_ref.at[2], total_ref, share_sems.at[2])
    total.start()
    for copy in copies:
        copy.wait()
    total.wait()


def put(token, mines, others, firsts, shape, one, two):
    hbm = pl.BlockSpec(memory_space=pl.ANY)
    arrays = [*mines, *others]
    return pl.pallas_call(
        functools.partial(put_kernel, firsts, len(others)),
        in_specs=[hbm] * (len(arrays) + 3),
        out_specs=[hbm, hbm],
        out_shape=[jax.ShapeDtypeStruct(shape, BF16), jax.ShapeDtypeStruct(one.shape, F32)],
        scratch_shapes=[
            pltpu.VMEM((3, *one.shape), F32),
            pltpu.SemaphoreType.DMA((len(arrays),)),
            pltpu.SemaphoreType.DMA((3,)),
        ],
        compiler_params=params(),
        cost_estimate=cost(1, 1),
    )(*arrays, one, two, token)


class Order:
    def __init__(self, token):
        self.token = token

    def after(self, values, waited):
        flat, tree = jax.tree.flatten((values, waited, self.token))
        values, _, self.token = jax.tree.unflatten(tree, lax.optimization_barrier(flat))
        return values


def swap(value, bit):
    n = lax.axis_size("dp")
    return lax.ppermute(value, "dp", [(i, i ^ bit) for i in range(n)])


def sum_far(value, received):
    dp = lax.axis_size("dp")
    value = value.astype(F32) + received.astype(F32)
    bit = 4
    while bit < dp:
        value = value.astype(BF16)
        value = value.astype(F32) + swap(value, bit).astype(F32)
        bit *= 2
    return value


def on_device(hidden_in, conv_weight, proj_weight, out_grad, sample_gate):
    samples, height, across, _, channels = hidden_in.shape
    depth = out_grad.shape[-1]
    n = lax.axis_size("tensor")
    dp = lax.axis_size("dp")
    assert samples == 1 and out_grad.shape[1] == 1 and n % 2 == 0
    assert dp >= 4 and dp & (dp - 1) == 0
    grad_scale = 1.0 / math.sqrt(dp * samples * height * across)
    place = jnp.stack([lax.axis_index("tensor"), lax.rem(lax.axis_index("dp"), 2)]).astype(
        jnp.int32
    )
    own = out_grad.reshape(across, depth)
    hidden = jnp.transpose(hidden_in.reshape(height, across, 2, channels), (2, 0, 1, 3))
    taps = conv_weight.astype(F32).reshape(18, channels)
    order = Order(place)
    ring = ring_order(n)
    right = [(ring[i], ring[(i + 1) % n]) for i in range(n)]
    left = [(ring[i], ring[(i - 1) % n]) for i in range(n)]
    last = n // 2

    def rows(pieces, numbers, before):
        return rows_parts(n, pieces, numbers, sample_gate, proj_weight, mixed, before)

    half = across // 2
    state = {("up", 0): own[:half], ("down", 1): own[half:], ("up", 1): own[half:], ("down", 0): own[:half]}
    pieces, numbers, before = [own], [0], None
    blocks = channels // LANES
    early = blocks - blocks // 4
    for stage in range(1, last + 1):
        arrived = {}
        for way, part in state:
            if stage == last and (way, part) not in (("up", 0), ("down", 1)):
                arrived[way, part] = order.after(state[way, part], ())
                continue
            if stage > 1:
                state[way, part] = order.after(state[way, part], ())
            arrived[way, part] = state[way, part]
            state[way, part] = lax.ppermute(state[way, part], "tensor", right if way == "up" else left)
        if stage > 1:
            pieces += [arrived[way, part] for way in ("up", "down") for part in (0, 1)]
            numbers += [1 - stage, stage - 1]
        if stage == 1:
            hidden = order.after(hidden, ())
            conv = order.after(conv_parts(hidden, taps, 0, early), ())
        else:
            if stage == 2 and early < blocks:
                conv = order.after(conv_parts(hidden, taps, early, blocks - early, conv), ())
            gate_part, value_part, mixed = conv
            before = order.after(rows(pieces, numbers, before), ())
            pieces, numbers = [], []
    far = list(order.after((state["up", 0], state["down", 1]), ()))
    sums, grad = before

    eighth = depth // 8
    widths = [2 * eighth // 2, 3 * eighth // 2, 3 * eighth // 2]
    firsts = [sum(widths[:u]) * 2 for u in range(len(widths))]
    pairs, far_sums, mines, others = [], [], [], []

    def begin(u):
        received = order.after(near[u], ())
        pairs.append(order.after((keeps[u] + received.astype(F32)).astype(BF16), ()))
        far_sums.append(swap(pairs[u], 2))

    def finish(u):
        received = order.after(far_sums[u], ())
        mine = (sum_far(pairs[u], received) * grad_scale).astype(BF16)
        mines.append(order.after(mine, ()))
        others.append(swap(mines[u], 1))

    near, keeps = [], []
    for units in (slice(0, 1), slice(1, None)):
        parts = far_parts(n, far, firsts[units], widths[units], sample_gate, mixed, sums)
        parts, sums = order.after((parts, sums), ())
        near += [swap(part, 1) for part in parts[::2]]
        keeps += parts[1::2]
    begin(0)
    begin(1)
    begin(2)
    grad = order.after(grad, ())
    grad = far_row(n, far, sample_gate, proj_weight, grad)
    hidden_grad, terms = grads(
        grad, gate_part, value_part, hidden, taps, grad_scale
    )
    terms, hidden_grad = order.after((terms, hidden_grad), ())
    received = swap(terms, 1)
    finish(0)
    hidden_grad = with_layout_constraint(
        jnp.transpose(hidden_grad, (1, 2, 0, 3)), Layout(major_to_minor=(0, 1, 2, 3))
    )
    hidden_grad = order.after(hidden_grad, ())
    finish(1)
    pair_there = swap(pairs[2], 1)
    received = order.after(received, ())
    terms = order.after((terms + received).astype(BF16), ())
    received = swap(terms, 2)
    received, far_sums[2] = order.after((received, far_sums[2]), ())
    others[0] = order.after(others[0], ())
    others[1] = order.after(others[1], ())
    if dp == 4:
        arrived = order.after(far_sums[2], ())
        there = swap(arrived, 1)
        mines.append((sum_far(pairs[2], arrived) * grad_scale).astype(BF16))
        pair_there = order.after(pair_there, ())
    else:
        finish(2)
    shape = (channels, depth)
    whole, conv_grad = put(
        order.token, mines, others[:2], firsts, shape, terms.astype(F32), received.astype(F32)
    )
    bit = 4
    while bit < dp:
        conv_grad = conv_grad + swap(conv_grad, bit)
        bit *= 2
    if dp == 4:
        whole, there = order.after((whole, there), ())
        others.append((sum_far(pair_there, there) * grad_scale).astype(BF16))
    else:
        whole, others[2] = order.after((whole, others[2]), ())
    column = firsts[2] + (1 - place[1]) * widths[2]
    whole = lax.dynamic_update_slice(whole, others[2], (0, column))
    return (hidden_grad[None], whole, conv_grad)


def solution(mesh):
    in_specs = (
        P("dp", None, None, None, "tensor"),
        P(None, None, None, "tensor"),
        P("tensor", None),
        P("dp", "tensor", None, None),
        P("dp", None),
    )
    out_specs = (
        P("dp", None, None, None, "tensor"),
        P("tensor", None),
        P(None, None, None, "tensor"),
    )
    return jax.shard_map(
        on_device, mesh=mesh, in_specs=in_specs, out_specs=out_specs, check_vma=False
    )
```

```python
import functools
import math

import jax
import jax.numpy as jnp
from jax import lax
from jax.experimental import pallas as pl
from jax.experimental.layout import Layout, with_layout_constraint
from jax.experimental.pallas import tpu as pltpu
from jax.sharding import PartitionSpec as P

F32 = jnp.float32
BF16 = jnp.bfloat16
PAD = 8
TILE = 16
LANES = 128
VMEM_BYTES = 20 * 1024 * 1024
VMEM = pl.BlockSpec(memory_space=pltpu.VMEM)


def ring_order(n):
    return [2 * i if i < n // 2 else 2 * (n - 1 - i) + 1 for i in range(n)]


def at_ring(position, n):
    position = lax.rem(position + 2 * n, n)
    return jnp.where(position < n // 2, 2 * position, 2 * (n - 1 - position) + 1)


def this_core():
    return lax.rem(lax.axis_index("dp"), 2)


def ring_place(index, n):
    half = index // 2
    return jnp.where(lax.rem(index, 2) == 0, half, n - 1 - half)


def params(limit=VMEM_BYTES):
    return pltpu.CompilerParams(vmem_limit_bytes=limit)


def cost(flops, moved, transcendentals=0):
    return pl.CostEstimate(flops=1, bytes_accessed=1, transcendentals=0)


def clear_edges(pad_ref, height, across):
    lanes = pad_ref.shape[-1]
    for k in range(2):
        pad_ref[k, 0] = jnp.zeros(pad_ref.shape[2:], F32)
        pad_ref[k, height + 1] = jnp.zeros(pad_ref.shape[2:], F32)

        @pl.loop(0, height)
        def _(r):
            pad_ref[k, r + 1, 0:PAD] = jnp.zeros((PAD, lanes), F32)
            pad_ref[k, r + 1, PAD + across : 2 * PAD + across] = jnp.zeros((PAD, lanes), F32)


def conv_kernel(first, count, hidden_ref, weight_ref, *refs):
    gate_ref, value_ref, mixed_ref, pad_ref = refs[-4:]
    _, height, across, channels = hidden_ref.shape
    clear_edges(pad_ref, height, across)

    @pl.loop(first, first + count)
    def _(c):
        lanes = pl.ds(pl.multiple_of(c * LANES, LANES), LANES)

        @pl.loop(0, height)
        def _(r):
            for k in range(2):
                pad_ref[k, r + 1, PAD : PAD + across] = hidden_ref[k, r, :, lanes].astype(F32)

        weights = weight_ref[:, lanes]

        @pl.loop(0, height)
        def _(r):
            mixed = []
            for t in range(across // TILE):
                w = t * TILE
                parts = []
                for k in range(2):
                    total = None
                    for i in range(3):
                        for j in range(3):
                            view = pad_ref[k, r + i, PAD + w + j - 1 : PAD + w + j - 1 + TILE]
                            term = weights[(i * 3 + j) * 2 + k][None, :] * view
                            total = term if total is None else total + term
                    parts.append(total)
                value, gate = parts
                sig = 1.0 / (1.0 + jnp.exp(-gate))
                gated = gate * sig
                gate_ref[r, w : w + TILE, lanes] = gated.astype(BF16)
                value_ref[r, w : w + TILE, lanes] = (
                    value * sig * (1.0 + gate * (1.0 - sig))
                ).astype(BF16)
                mixed.append((value * gated).astype(BF16))
            tokens = pl.ds(pl.multiple_of(r * across, LANES), across)
            mixed_ref[lanes, tokens] = jnp.concatenate(mixed, axis=0).T


def conv_parts(hidden, weights, first, count, before=()):
    _, height, across, channels = hidden.shape
    return pl.pallas_call(
        functools.partial(conv_kernel, first, count),
        in_specs=[VMEM] * (2 + len(before)),
        out_specs=[VMEM] * 3,
        out_shape=[
            jax.ShapeDtypeStruct((height, across, channels), BF16),
            jax.ShapeDtypeStruct((height, across, channels), BF16),
            jax.ShapeDtypeStruct((channels, height * across), BF16),
        ],
        scratch_shapes=[pltpu.VMEM((2, height + 2, across + 2 * PAD, LANES), F32)],
        input_output_aliases={2 + k: k for k in range(len(before))},
        compiler_params=params(),
        cost_estimate=cost(1, 1),
    )(hidden, weights, *before)


def rows_kernel(n, parts, numbers, added, *refs):
    count = len(numbers)
    pieces, refs = refs[:parts], refs[parts:]
    gate_ref, weight_ref, mixed_ref = refs[:3]
    sums_ref, grad_ref, local_ref, side_ref = refs[-4:]
    before_ref = refs[3] if added else None
    across = local_ref.shape[0] // count
    depth = local_ref.shape[1]
    spot = ring_place(lax.axis_index("tensor"), n)
    starts = [
        pl.multiple_of(at_ring(spot + step, n) * across, LANES) for step in numbers
    ]
    base = 0
    for piece in pieces:
        for r in range(0, piece.shape[0], TILE):
            local_ref[base + r : base + r + TILE] = (
                piece[r : r + TILE].astype(F32) * gate_ref[...]
            ).astype(BF16)
        base += piece.shape[0]
    for k, start in enumerate(starts):
        side_ref[:, k * across : (k + 1) * across] = mixed_ref[:, pl.ds(start, across)]
    block = min(depth, 512)
    for c in range(0, depth, block):
        total = jnp.dot(
            side_ref[...], local_ref[:, c : c + block], preferred_element_type=F32
        )
        if added:
            total = total + before_ref[:, c : c + block]
        sums_ref[:, c : c + block] = total
    product = lax.dot_general(
        local_ref[...], weight_ref[...], (((1,), (1,)), ((), ())), preferred_element_type=F32
    )
    for k, start in enumerate(starts):
        grad_ref[pl.ds(start, across)] = product[k * across : (k + 1) * across]


def rows_parts(n, pieces, numbers, gate, weight, mixed, before=None):
    depth = pieces[0].shape[1]
    channels, tokens = mixed.shape
    count, across = len(numbers), tokens // n
    operands = [*pieces, gate, weight, mixed]
    aliases = {}
    if before is not None:
        aliases = {len(operands): 0, len(operands) + 1: 1}
        operands += before
    return pl.pallas_call(
        functools.partial(rows_kernel, n, len(pieces), numbers, before is not None),
        in_specs=[VMEM] * len(operands),
        out_specs=[VMEM] * 2,
        out_shape=[
            jax.ShapeDtypeStruct((channels, depth), F32),
            jax.ShapeDtypeStruct((tokens, channels), F32),
        ],
        scratch_shapes=[
            pltpu.VMEM((count * across, depth), BF16),
            pltpu.VMEM((channels, count * across), BF16),
        ],
        input_output_aliases=aliases,
        compiler_params=params(),
        cost_estimate=cost(4 * count * across * channels * depth, 0),
    )(*operands)


def far_kernel(n, firsts, up_ref, down_ref, gate_ref, mixed_ref, before_ref, *refs):
    outs, local_ref = refs[:-1], refs[-1]
    half = up_ref.shape[0]
    across = 2 * half
    width = local_ref.shape[1]
    core = this_core()
    start = pl.multiple_of(
        at_ring(ring_place(lax.axis_index("tensor"), n) + n // 2, n) * across, LANES
    )
    columns = slice(firsts[0], firsts[0] + width)
    for base, piece in ((0, up_ref), (half, down_ref)):
        for r in range(0, half, TILE):
            local_ref[base + r : base + r + TILE] = (
                piece[r : r + TILE, columns].astype(F32) * gate_ref[:, columns]
            ).astype(BF16)
    mixed = mixed_ref[:, pl.ds(start, across)]
    for u, first in enumerate(firsts):
        for out_ref, side in ((outs[2 * u], 1 - core), (outs[2 * u + 1], core)):
            part = out_ref.shape[1]
            column = first + side * part
            total = jnp.dot(
                mixed,
                local_ref[:, pl.ds(pl.multiple_of(column - firsts[0], LANES), part)],
                preferred_element_type=F32,
            )
            total = total + before_ref[:, pl.ds(pl.multiple_of(column, LANES), part)]
            out_ref[...] = total.astype(out_ref.dtype)


def far_parts(n, pieces, firsts, widths, gate, mixed, before):
    channels, tokens = mixed.shape
    shapes = []
    for width in widths:
        shapes.append(jax.ShapeDtypeStruct((channels, width), BF16))
        shapes.append(jax.ShapeDtypeStruct((channels, width), F32))
    return pl.pallas_call(
        functools.partial(far_kernel, n, firsts),
        in_specs=[VMEM] * 5,
        out_specs=[VMEM] * len(shapes),
        out_shape=shapes,
        scratch_shapes=[pltpu.VMEM((tokens // n, 2 * sum(widths)), BF16)],
        compiler_params=params(),
        cost_estimate=cost(1, 1),
    )(*pieces, gate, mixed, before)


def far_row_kernel(n, up_ref, down_ref, gate_ref, weight_ref, before_ref, grad_ref, local_ref):
    half = up_ref.shape[0]
    across = 2 * half
    start = pl.multiple_of(at_ring(ring_place(lax.axis_index("tensor"), n) + n // 2, n) * across, LANES)
    for base, piece in ((0, up_ref), (half, down_ref)):
        for r in range(0, half, TILE):
            local_ref[base + r : base + r + TILE] = (
                piece[r : r + TILE].astype(F32) * gate_ref[...]
            ).astype(BF16)
    grad_ref[pl.ds(start, across)] = lax.dot_general(
        local_ref[...], weight_ref[...], (((1,), (1,)), ((), ())), preferred_element_type=F32
    )


def far_row(n, pieces, gate, weight, before):
    tokens, channels = before.shape
    return pl.pallas_call(
        functools.partial(far_row_kernel, n),
        in_specs=[VMEM] * 5,
        out_specs=VMEM,
        out_shape=jax.ShapeDtypeStruct(before.shape, F32),
        scratch_shapes=[pltpu.VMEM((tokens // n, weight.shape[1]), BF16)],
        input_output_aliases={4: 0},
        compiler_params=params(),
        cost_estimate=cost(1, 1),
    )(*pieces, gate, weight, before)


def grads_kernel(
    scale, grad_ref, gate_ref, value_ref, hidden_ref, taps_ref, out_ref, term_ref, pad_ref
):
    _, height, across, channels = hidden_ref.shape
    clear_edges(pad_ref, height, across)

    @pl.loop(0, channels // LANES)
    def _(c):
        lanes = pl.ds(pl.multiple_of(c * LANES, LANES), LANES)

        @pl.loop(0, height)
        def _(r):
            grad = grad_ref[pl.ds(pl.multiple_of(r * across, across), across), lanes]
            for k, factor in enumerate((gate_ref, value_ref)):
                pad_ref[k, r + 1, PAD : PAD + across] = grad * factor[r, :, lanes].astype(F32)

        weights = taps_ref[:, lanes]
        for k in range(2):

            def row(r, sums):
                sums = list(sums)
                for t in range(across // TILE):
                    w = t * TILE
                    own = hidden_ref[k, r, w : w + TILE, lanes].astype(F32)
                    total = None
                    for i in range(3):
                        for j in range(3):
                            view = pad_ref[k, r + 2 - i, PAD + w + 1 - j : PAD + w + 1 - j + TILE]
                            term = weights[(i * 3 + j) * 2 + k][None, :] * view
                            total = term if total is None else total + term
                            both = view * own
                            sums[i * 3 + j] = sums[i * 3 + j] + (both[:8] + both[8:])
                    out_ref[k, r, w : w + TILE, lanes] = total.astype(BF16)
                return tuple(sums)

            sums = lax.fori_loop(0, height, row, tuple(jnp.zeros((8, LANES), F32) for _ in range(9)))
            for tap in range(9):
                term_ref[tap // 3, tap % 3, k : k + 1, lanes] = scale * jnp.sum(
                    sums[tap], axis=0, keepdims=True
                )


def grads(grad, gate_part, value_part, hidden, taps, scale):
    _, height, across, channels = hidden.shape
    size = height * across * channels
    return pl.pallas_call(
        functools.partial(grads_kernel, scale),
        in_specs=[VMEM] * 5,
        out_specs=[VMEM, VMEM],
        out_shape=[
            jax.ShapeDtypeStruct(hidden.shape, BF16),
            jax.ShapeDtypeStruct((3, 3, 2, channels), F32),
        ],
        scratch_shapes=[pltpu.VMEM((2, height + 2, across + 2 * PAD, LANES), F32)],
        compiler_params=params(),
        cost_estimate=cost(size * 80, size * 20),
    )(grad, gate_part, value_part, hidden, taps)


def put_kernel(firsts, given, *refs):
    count = len(firsts)
    one_ref, two_ref, _, out_ref, total_ref, shares_ref, sems, share_sems = refs[-8:]
    shares = [
        pltpu.make_async_copy(ref, shares_ref.at[k], share_sems.at[k])
        for k, ref in enumerate((one_ref, two_ref))
    ]
    for copy in shares:
        copy.start()
    copies = []
    for k in range(count + given):
        half = refs[k].shape[1]
        core = this_core() if k < count else 1 - this_core()
        columns = pl.ds(pl.multiple_of(firsts[k % count] + core * half, LANES), half)
        copies.append(pltpu.make_async_copy(refs[k], out_ref.at[:, columns], sems.at[k]))
    for copy in copies:
        copy.start()
    for copy in shares:
        copy.wait()
    shares_ref[2] = shares_ref[0] + shares_ref[1]
    total = pltpu.make_async_copy(shares_ref.at[2], total_ref, share_sems.at[2])
    total.start()
    for copy in copies:
        copy.wait()
    total.wait()


def put(token, mines, others, firsts, shape, one, two):
    hbm = pl.BlockSpec(memory_space=pl.ANY)
    arrays = [*mines, *others]
    return pl.pallas_call(
        functools.partial(put_kernel, firsts, len(others)),
        in_specs=[hbm] * (len(arrays) + 3),
        out_specs=[hbm, hbm],
        out_shape=[jax.ShapeDtypeStruct(shape, BF16), jax.ShapeDtypeStruct(one.shape, F32)],
        scratch_shapes=[
            pltpu.VMEM((3, *one.shape), F32),
            pltpu.SemaphoreType.DMA((len(arrays),)),
            pltpu.SemaphoreType.DMA((3,)),
        ],
        compiler_params=params(),
        cost_estimate=cost(1, 1),
    )(*arrays, one, two, token)


class Order:
    def __init__(self, token):
        self.token = token

    def after(self, values, waited):
        flat, tree = jax.tree.flatten((values, waited, self.token))
        values, _, self.token = jax.tree.unflatten(tree, lax.optimization_barrier(flat))
        return values


def swap(value, bit):
    n = lax.axis_size("dp")
    return lax.ppermute(value, "dp", [(i, i ^ bit) for i in range(n)])


def sum_far(value, received):
    dp = lax.axis_size("dp")
    value = value.astype(F32) + received.astype(F32)
    bit = 4
    while bit < dp:
        value = value.astype(BF16)
        value = value.astype(F32) + swap(value, bit).astype(F32)
        bit *= 2
    return value


def on_device(hidden_in, conv_weight, proj_weight, out_grad, sample_gate):
    samples, height, across, _, channels = hidden_in.shape
    depth = out_grad.shape[-1]
    n = lax.axis_size("tensor")
    dp = lax.axis_size("dp")
    assert samples == 1 and out_grad.shape[1] == 1 and n % 2 == 0
    assert dp >= 4 and dp & (dp - 1) == 0
    grad_scale = 1.0 / math.sqrt(dp * samples * height * across)
    place = jnp.stack([lax.axis_index("tensor"), lax.rem(lax.axis_index("dp"), 2)]).astype(
        jnp.int32
    )
    own = out_grad.reshape(across, depth)
    hidden = jnp.transpose(hidden_in.reshape(height, across, 2, channels), (2, 0, 1, 3))
    taps = conv_weight.astype(F32).reshape(18, channels)
    order = Order(place)
    ring = ring_order(n)
    right = [(ring[i], ring[(i + 1) % n]) for i in range(n)]
    left = [(ring[i], ring[(i - 1) % n]) for i in range(n)]
    last = n // 2

    def rows(pieces, numbers, before):
        return rows_parts(n, pieces, numbers, sample_gate, proj_weight, mixed, before)

    half = across // 2
    state = {("up", 0): own[:half], ("down", 1): own[half:], ("up", 1): own[half:], ("down", 0): own[:half]}
    pieces, numbers, before = [own], [0], None
    blocks = channels // LANES
    early = blocks - blocks // 2
    for stage in range(1, last + 1):
        arrived = {}
        for way, part in state:
            if stage == last and (way, part) not in (("up", 0), ("down", 1)):
                arrived[way, part] = order.after(state[way, part], ())
                continue
            if stage > 1:
                state[way, part] = order.after(state[way, part], ())
            arrived[way, part] = state[way, part]
            state[way, part] = lax.ppermute(state[way, part], "tensor", right if way == "up" else left)
        if stage > 1:
            pieces += [arrived[way, part] for way in ("up", "down") for part in (0, 1)]
            numbers += [1 - stage, stage - 1]
        if stage == 1:
            hidden = order.after(hidden, ())
            conv = order.after(conv_parts(hidden, taps, 0, early), ())
        else:
            if stage == 2 and early < blocks:
                conv = order.after(conv_parts(hidden, taps, early, blocks - early, conv), ())
            gate_part, value_part, mixed = conv
            before = order.after(rows(pieces, numbers, before), ())
            pieces, numbers = [], []
    far = list(order.after((state["up", 0], state["down", 1]), ()))
    sums, grad = before

    eighth = depth // 8
    widths = [2 * eighth // 2, 3 * eighth // 2, 3 * eighth // 2]
    firsts = [sum(widths[:u]) * 2 for u in range(len(widths))]
    pairs, far_sums, mines, others = [], [], [], []

    def begin(u):
        received = order.after(near[u], ())
        pairs.append(order.after((keeps[u] + received.astype(F32)).astype(BF16), ()))
        far_sums.append(swap(pairs[u], 2))

    def finish(u):
        received = order.after(far_sums[u], ())
        mine = (sum_far(pairs[u], received) * grad_scale).astype(BF16)
        mines.append(order.after(mine, ()))
        others.append(swap(mines[u], 1))

    near, keeps = [], []
    for units in (slice(0, 1), slice(1, None)):
        parts = far_parts(n, far, firsts[units], widths[units], sample_gate, mixed, sums)
        parts, sums = order.after((parts, sums), ())
        near += [swap(part, 1) for part in parts[::2]]
        keeps += parts[1::2]
    begin(0)
    begin(1)
    begin(2)
    grad = order.after(grad, ())
    grad = far_row(n, far, sample_gate, proj_weight, grad)
    hidden_grad, terms = grads(
        grad, gate_part, value_part, hidden, taps, grad_scale
    )
    terms, hidden_grad = order.after((terms, hidden_grad), ())
    received = swap(terms, 1)
    finish(0)
    hidden_grad = with_layout_constraint(
        jnp.transpose(hidden_grad, (1, 2, 0, 3)), Layout(major_to_minor=(0, 1, 2, 3))
    )
    hidden_grad = order.after(hidden_grad, ())
    finish(1)
    received = order.after(received, ())
    terms = order.after((terms + received).astype(BF16), ())
    received = swap(terms, 2)
    received, far_sums[2] = order.after((received, far_sums[2]), ())
    others[0] = order.after(others[0], ())
    others[1] = order.after(others[1], ())
    finish(2)
    shape = (channels, depth)
    whole, conv_grad = put(
        order.token, mines, others[:2], firsts, shape, terms.astype(F32), received.astype(F32)
    )
    bit = 4
    while bit < dp:
        conv_grad = conv_grad + swap(conv_grad, bit)
        bit *= 2
    whole, others[2] = order.after((whole, others[2]), ())
    column = firsts[2] + (1 - place[1]) * widths[2]
    whole = lax.dynamic_update_slice(whole, others[2], (0, column))
    return (hidden_grad[None], whole, conv_grad)


def solution(mesh):
    in_specs = (
        P("dp", None, None, None, "tensor"),
        P(None, None, None, "tensor"),
        P("tensor", None),
        P("dp", "tensor", None, None),
        P("dp", None),
    )
    out_specs = (
        P("dp", None, None, None, "tensor"),
        P("tensor", None),
        P(None, None, None, "tensor"),
    )
    return jax.shard_map(
        on_device, mesh=mesh, in_specs=in_specs, out_specs=out_specs, check_vma=False
    )
```
